512 devices in a mesh: pipe: 32 (over x, y), expert: 16 (over z, core).
Axes of the slice: x: 4, y: 8, z: 8, core: 2. Of those that a mesh axis runs over, the one named last changes fastest.
Arguments:
- first_state: bfloat16 [32, 512, 3584], P('pipe', 'expert'), may hold values from -6 to 6
- second_state: bfloat16 [32, 512, 3584], P('pipe', 'expert'), may hold values from -6 to 6
- first_enter: bfloat16 [1, 512, 3584], P(None, 'expert'), may hold values from -6 to 6
- second_enter: bfloat16 [1, 512, 3584], P(None, 'expert'), may hold values from -6 to 6
- norm_gain: float32 [32, 3584], P('pipe'), may hold values from 0.5 to 1.5
- router: float32 [32, 3584, 2], P('pipe'), may hold values from -0.09375 to 0.09375
- gate_proj: bfloat16 [32, 3584, 2048], P('pipe', None, 'expert'), may hold values from -0.09375 to 0.09375
- up_proj: bfloat16 [32, 3584, 2048], P('pipe', None, 'expert'), may hold values from -0.09375 to 0.09375
- down_proj: bfloat16 [32, 2048, 3584], P('pipe', 'expert'), may hold values from -0.1875 to 0.1875
- first_routes: int32 [2, 32, 512, 1], P(None, 'pipe', 'expert'), may hold values from 0 to 1; in each aligned block of 32 rows (0 to 31, 32 to 63, ..., all dimensions but the last counted through in order) at most 17 rows name the same one
- second_routes: int32 [2, 32, 512, 1], P(None, 'pipe', 'expert'), may hold values from 0 to 1; in each aligned block of 32 rows (0 to 31, 32 to 63, ..., all dimensions but the last counted through in order) at most 17 rows name the same one
Outputs:
- first_out: bfloat16 [2, 32, 512, 3584], P(None, 'pipe', 'expert')
- second_out: bfloat16 [2, 32, 512, 3584], P(None, 'pipe', 'expert')
The draws below stay inside these ranges and needn't reach their ends.
Inputs may be any that keep to these rules, and one draw needn't show every extreme that they name: `first_routes`: within the 32 rows of one device at one step and section no expert is named by more than 17 rows, a bound that some block reaches. `second_routes`: within the 32 rows of one device at one step and section no expert is named by more than 17 rows, a bound that some block reaches.
All inputs are finite; a program needn't handle non-finite values.
Results may differ from the reference program's by a relative error of at most 0.0067.
Values may be sent and summed in bfloat16 or wider, within the bound.
A program may use at most 64 MiB of HBM per device.

```python
import math
import jax
import jax.numpy as jnp
import numpy as np
from jax import lax

D = 3584
FF = 1024
EXP_WIN = 2
TOP = 1
STEPS = 2
TOK = 32
CAP = 17
ROWS = 512
FF_DEV = 128
SECTIONS = 32
N_EXPERT = 16


def shard_levels(rng, extent, shards, smallest, high):
    level, own = 1.0, jax.random.fold_in(rng, 6)
    for position, parts in shards:
        heights = jnp.exp(jax.random.uniform(jax.random.fold_in(own, position), (parts,), jnp.float32, smallest / len(shards), high / len(shards)))
        level = level * jnp.repeat(heights, extent[position] // parts).reshape([-1 if axis == position else 1 for axis in range(len(extent))])
    return level


def assign_block(key, own, number, rows, number_of, top, limit, lean):
    ranking = jax.random.permutation(key, number_of)
    crowded, common = load_shares(number_of, rows * top, limit, lean, True), load_shares(number_of, rows * top, limit, lean, False)
    places = jnp.arange(number_of)

    def named(tallies, offset_by):
        used = int((tallies > 0).sum())
        fixed = max(1, used // 4)
        passed = fixed + (places - fixed + offset_by * (used - fixed)) % max(1, number_of - fixed)
        return jnp.zeros((number_of,), jnp.int32).at[ranking[jnp.where(places < fixed, places, passed)]].set(jnp.asarray(tallies, jnp.int32))

    tallies = jnp.where(number % 4 == 0, named(crowded, number // 4), named(common, number - number // 4 - 1))
    mixed = jax.random.permutation(jax.random.fold_in(own, 3), number_of)
    source_of, receiver = mixed[0:number_of // 2 * 2:2], mixed[1:number_of // 2 * 2:2]
    margin = jnp.minimum(tallies[source_of] - 1, limit - tallies[receiver]) // 2
    margin = jnp.where((source_of == ranking[0]) | (receiver == ranking[0]) | (tallies[receiver] == 0), 0, jnp.maximum(margin, 0))
    passed = jax.random.randint(jax.random.fold_in(own, 4), (number_of // 2,), 0, 1 << 20) % (margin + 1)
    tallies = tallies.at[source_of].add(-passed).at[receiver].add(passed)
    labels = jnp.searchsorted(jnp.cumsum(tallies), jnp.arange(rows * top), side="right").astype(jnp.int32)
    table = labels.reshape(top, rows).T
    table = table[jax.random.permutation(jax.random.fold_in(own, 1), rows)]
    offset_by = jax.random.randint(jax.random.fold_in(own, 2), (rows, 1), 0, top)
    return jnp.take_along_axis(table, (jnp.arange(top)[None, :] + offset_by) % top, axis=1)


def load_shares(amount, total, bound, slope, full):
    loads = [(1 << 20) // math.isqrt(grade ** slope) + 1 for grade in range(1, amount + 1)]
    largest = bound if full else min(bound, max(-(-total // amount), total * loads[0] // sum(loads)))
    least = 1 if total - largest >= amount - 1 else 0
    holding, rest = [largest] + [least] * (amount - 1), total - largest - least * (amount - 1)
    while rest > 0:
        free = [i for i in range(1, amount) if holding[i] < largest] or [i for i in range(1, amount) if holding[i] < bound]
        pool, budget = sum([loads[i] for i in free]), rest
        for i in free:
            more = min(bound - holding[i], max(1, budget * loads[i] // pool), rest)
            holding[i] = holding[i] + more
            rest = rest - more
    return np.array(holding)


def scatter_about(key, extent, deviation, reach, pieces=(), held_as=jnp.bfloat16):
    result = deviation * jax.random.normal(key, extent, jnp.float32)
    if pieces:
        result = result * shard_levels(key, extent, pieces, -0.22, 0.18)
    return jnp.clip(result, -reach, reach).astype(held_as)


def setup_inputs(seed: int = 0) -> dict:
    seeds = jax.random.split(jax.random.key(seed), 12)
    first_state = scatter_about(seeds[0], (SECTIONS, ROWS, D), 1.0, 6.0, ((0, 32), (1, 16)))
    second_state = scatter_about(seeds[1], (SECTIONS, ROWS, D), 1.0, 6.0, ((0, 32), (1, 16)))
    first_enter = scatter_about(seeds[2], (STEPS - 1, ROWS, D), 1.0, 6.0, ((1, 16),))
    second_enter = scatter_about(seeds[3], (STEPS - 1, ROWS, D), 1.0, 6.0, ((1, 16),))
    norm_gain = jnp.clip(1.0 + 0.1 * jax.random.normal(seeds[4], (SECTIONS, D), jnp.float32), 0.5, 1.5)
    router = scatter_about(seeds[5], (SECTIONS, D, EXP_WIN), D ** -0.5, 0.09375, ((0, 32),), jnp.float32)
    gate_proj = scatter_about(seeds[6], (SECTIONS, D, EXP_WIN * FF), D ** -0.5, 0.09375, ((0, 32), (2, 16)))
    up_proj = scatter_about(seeds[7], (SECTIONS, D, EXP_WIN * FF), D ** -0.5, 0.09375, ((0, 32), (2, 16)))
    down_proj = scatter_about(seeds[8], (SECTIONS, EXP_WIN * FF, D), FF ** -0.5, 0.1875, ((0, 32), (1, 16)))
    first_routes_keys = jax.random.split(jax.random.fold_in(seeds[9], 1), STEPS * SECTIONS * ROWS // TOK)
    first_routes_turns = jax.random.permutation(jax.random.fold_in(seeds[9], 3), STEPS * SECTIONS * ROWS // TOK)
    first_routes = jax.vmap(lambda own, number: assign_block(jax.random.fold_in(seeds[9], 2), own, number, TOK, EXP_WIN, TOP, CAP, 1))(first_routes_keys, first_routes_turns).reshape((STEPS, SECTIONS, ROWS, TOP))
    second_routes_keys = jax.random.split(jax.random.fold_in(seeds[10], 1), STEPS * SECTIONS * ROWS // TOK)
    second_routes_turns = jax.random.permutation(jax.random.fold_in(seeds[10], 3), STEPS * SECTIONS * ROWS // TOK)
    second_routes = jax.vmap(lambda own, number: assign_block(jax.random.fold_in(seeds[10], 2), own, number, TOK, EXP_WIN, TOP, CAP, 1))(second_routes_keys, second_routes_turns).reshape((STEPS, SECTIONS, ROWS, TOP))
    return dict(first_state=first_state, second_state=second_state, first_enter=first_enter, second_enter=second_enter, norm_gain=norm_gain, router=router, gate_proj=gate_proj, up_proj=up_proj, down_proj=down_proj, first_routes=first_routes, second_routes=second_routes)


epsilon = 1e-06
route_scale = 2.5

def section_apply(tokens, gains, router, gate_proj, up_proj, down_proj, route):
    widened = tokens.astype(jnp.float32)
    inverse = lax.rsqrt(lax.optimization_barrier(jnp.mean(widened * widened, axis=-1, keepdims=True)) + epsilon)
    normed = (widened * inverse * gains[None, :]).astype(jnp.bfloat16)
    scores = jnp.dot(normed.astype(jnp.float32), router, precision=lax.Precision.HIGHEST)
    chosen = route[:, 0]
    onehot = (chosen[:, None] == jnp.arange(EXP_WIN, dtype=jnp.int32)[None, :]).astype(jnp.float32)
    weight = route_scale * jax.nn.sigmoid(lax.optimization_barrier(jnp.sum(scores * onehot, axis=1)))
    gate_act = jnp.dot(normed, gate_proj, preferred_element_type=jnp.float32)
    up_act = jnp.dot(normed, up_proj, preferred_element_type=jnp.float32)
    hidden = (jax.nn.silu(gate_act) * up_act).astype(jnp.bfloat16)
    slices = hidden.reshape(hidden.shape[0], N_EXPERT, FF_DEV).astype(jnp.float32)
    downs = down_proj.reshape(N_EXPERT, FF_DEV, D).astype(jnp.float32)
    part_sum = jnp.einsum('tsf,sfd->tsd', slices, downs).astype(jnp.bfloat16)
    part_sum = lax.optimization_barrier(part_sum).astype(jnp.float32)
    owners = jnp.arange(N_EXPERT, dtype=jnp.int32) // (N_EXPERT // EXP_WIN)
    selected = (owners[None, :] == chosen[:, None]).astype(jnp.float32)
    expert_out = lax.optimization_barrier(jnp.sum(part_sum * selected[:, :, None], axis=1))
    return (widened + weight[:, None] * expert_out).astype(jnp.bfloat16)

def run_direction(state, enter, routes, gains, router, gate_proj, up_proj, down_proj, forward):

    def apply_all(blocks, step_routes):
        return lax.map(lambda packet: section_apply(*packet), (blocks, gains, router, gate_proj, up_proj, down_proj, step_routes))
    outputs = []
    current = state
    for step_index in range(STEPS):
        if step_index > 0:
            previous = outputs[-1]
            if forward:
                current = jnp.concatenate([enter[step_index - 1][None], previous[:-1]], axis=0)
            else:
                current = jnp.concatenate([previous[1:], enter[step_index - 1][None]], axis=0)
        outputs.append(apply_all(current, routes[step_index]))
    return jnp.stack(outputs)

def reference(first_state, second_state, first_enter, second_enter, norm_gain, router, gate_proj, up_proj, down_proj, first_routes, second_routes):
    first_out = run_direction(first_state, first_enter, first_routes, norm_gain, router, gate_proj, up_proj, down_proj, True)
    second_out = run_direction(second_state, second_enter, second_routes, norm_gain, router, gate_proj, up_proj, down_proj, False)
    return (first_out, second_out)
```

```python
import jax
import jax.numpy as jnp
from jax import lax
from jax.sharding import PartitionSpec as P

EXP_WIN = 2

epsilon = 1e-06
route_scale = 2.5


def passed_along(block, axis, distance):
    devices = range(lax.axis_size(axis))
    route = [(i - distance, i) for i in devices if i - distance in devices]
    return lax.ppermute(block, axis, route)


def normalize(tokens, gains):
    widened = tokens.astype(jnp.float32)
    inverse = lax.rsqrt(jnp.mean(widened * widened, axis=-1, keepdims=True) + epsilon)
    return (widened * inverse * gains[None, :]).astype(jnp.bfloat16)


def gate_weight(normed, router, route):
    scores = jnp.dot(normed.astype(jnp.float32), router, precision=lax.Precision.HIGHEST)
    onehot = (route == jnp.arange(EXP_WIN, dtype=jnp.int32)[None, :]).astype(jnp.float32)
    return route_scale * jax.nn.sigmoid(jnp.sum(scores * onehot, axis=1, keepdims=True))


def layer(tokens, route, all_routes, gains, router, both, down_proj, mine):
    normed = normalize(tokens, gains)
    everyone = lax.all_gather(normed, "expert", axis=0, tiled=True)
    weight = gate_weight(normed, router, route)
    acts = jnp.dot(everyone, both, preferred_element_type=jnp.float32)
    units = acts.shape[1] // 2
    hidden = jax.nn.silu(acts[:, :units]) * acts[:, units:]
    hidden = jnp.where(all_routes == mine, hidden, 0.0).astype(jnp.bfloat16)
    part = jnp.dot(hidden, down_proj, preferred_element_type=jnp.float32).astype(jnp.bfloat16)
    expert_out = lax.psum_scatter(part, "expert", scatter_dimension=0, tiled=True)
    return (tokens.astype(jnp.float32) + weight * expert_out.astype(jnp.float32)).astype(
        jnp.bfloat16
    )


def shards(
    first_state,
    second_state,
    first_enter,
    second_enter,
    norm_gain,
    router,
    gate_proj,
    up_proj,
    down_proj,
    first_routes,
    second_routes,
):
    gains = norm_gain[0]
    router_cols = router[0]
    both = jnp.concatenate([gate_proj[0], up_proj[0]], axis=1)
    down_local = down_proj[0]
    position = lax.axis_index("pipe")
    final_section = lax.axis_size("pipe") - 1
    mine = lax.axis_index("expert") // (lax.axis_size("expert") // EXP_WIN)
    routes = jnp.stack([first_routes[:, 0], second_routes[:, 0]])
    all_routes = lax.all_gather(routes, "expert", axis=2, tiled=True)
    now = [first_state[0], second_state[0]]
    done = [[], []]
    for step_index in range(first_routes.shape[0]):
        if step_index > 0:
            first_moved = passed_along(done[0][-1], "pipe", 1)
            second_moved = passed_along(done[1][-1], "pipe", -1)
            now = [
                jnp.where(position == 0, first_enter[step_index - 1], first_moved),
                jnp.where(position == final_section, second_enter[step_index - 1], second_moved),
            ]
        for which in range(2):
            done[which].append(
                layer(
                    now[which],
                    routes[which, step_index],
                    all_routes[which, step_index],
                    gains,
                    router_cols,
                    both,
                    down_local,
                    mine,
                )
            )
    return (jnp.stack(done[0])[:, None], jnp.stack(done[1])[:, None])


def solution(mesh):
    return jax.shard_map(
        shards,
        mesh=mesh,
        in_specs=(
            P("pipe", "expert", None),
            P("pipe", "expert", None),
            P(None, "expert", None),
            P(None, "expert", None),
            P("pipe", None),
            P("pipe", None, None),
            P("pipe", None, "expert"),
            P("pipe", None, "expert"),
            P("pipe", "expert", None),
            P(None, "pipe", "expert", None),
            P(None, "pipe", "expert", None),
        ),
        out_specs=(P(None, "pipe", "expert", None), P(None, "pipe", "expert", None)),
        check_vma=False,
    )
```

```python
import functools

import jax
import jax.numpy as jnp
from jax import lax
from jax.experimental import pallas as pl
from jax.experimental.pallas import tpu as pltpu
from jax.sharding import PartitionSpec as P

EXP_WIN = 2
MESH = pl.DeviceIdType.MESH

epsilon = 1e-06
route_scale = 2.5

BELOW = (1, 6, 4, 2, 0)
ABOVE = (1, 7, 5, 3, 0)
SLOTS = 8
CHUNKS = 4
GATHER_UP = ((0, 0), (0, 1), (1, 0), (1, 1), (2, 0), (2, 1), (3, 0))
GATHER_DOWN = ((0, 1), (0, 0), (1, 1), (1, 0), (2, 1), (2, 0), (3, 1))
REDUCE_UP = ((4, 0), (3, 1), (3, 0), (2, 1), (2, 0), (1, 1), (1, 0))
REDUCE_DOWN = ((4, 1), (3, 0), (3, 1), (2, 0), (2, 1), (1, 0), (1, 1))
UNITS = 7
LANES = 128


def relay_kernel(
    chips,
    sections,
    first_state,
    second_state,
    first_enter,
    second_enter,
    gains,
    router,
    gate_hbm,
    up_hbm,
    down_hbm,
    first_routes,
    second_routes,
    first_out,
    second_out,
    held,
    part,
    sib_part,
    from_below,
    from_above,
    arrived,
    current,
    weight,
    both,
    down,
    named,
    gu_s,
    gu_r,
    gd_s,
    gd_r,
    gs_s,
    gs_r,
    ru_s,
    ru_r,
    rd_s,
    rd_r,
    rs_s,
    rs_r,
    pipe_s,
    pipe_r,
    nu_s,
    nu_r,
    nd_s,
    nd_r,
    ns_s,
    ns_r,
    load_sem,
):
    rows, width = current.shape[1:]
    half_rows = rows // 2
    units = down.shape[0]
    e = lax.axis_index("expert")
    p = lax.axis_index("pipe")
    z, c = e // 2, e % 2
    mine = (z // (chips // EXP_WIN)).astype(jnp.float32)
    above = {"expert": ((z + 1) % chips) * 2 + c}
    below = {"expert": ((z + chips - 1) % chips) * 2 + c}
    sibling = {"expert": z * 2 + (1 - c)}
    onward = {"pipe": (p + 1) % sections}
    backward = {"pipe": (p + sections - 1) % sections}
    routes = (first_routes, second_routes)
    states = (first_state, second_state)
    enters = (first_enter, second_enter)
    outs = (first_out, second_out)

    def remote(src, dst, send, recv, device):
        return pltpu.make_async_remote_copy(
            src_ref=src,
            dst_ref=dst,
            send_sem=send,
            recv_sem=recv,
            device_id=device,
            device_id_type=MESH,
        )

    def half(index):
        return pl.ds(index * half_rows, half_rows)

    def gather_copy(t, s, j, up):
        d, h = (GATHER_UP if up else GATHER_DOWN)[j]
        slots = BELOW if up else ABOVE
        return remote(
            held.at[t, s, slots[d], c, half(h)],
            held.at[t, s, slots[d + 1], c, half(h)],
            (gu_s if up else gd_s).at[t, s, j],
            (gu_r if up else gd_r).at[t, s, j],
            above if up else below,
        )

    def gather_sibling(t, s, slot, core):
        ref = held.at[t, s, slot, core]
        return remote(ref, ref, gs_s.at[t, s, slot], gs_r.at[t, s, slot], sibling)

    def names_copy(d, up):
        slots = BELOW if up else ABOVE
        return remote(
            named.at[slots[d], c],
            named.at[slots[d + 1], c],
            (nu_s if up else nd_s).at[d],
            (nu_r if up else nd_r).at[d],
            above if up else below,
        )

    def names_sibling(slot, core):
        ref = named.at[slot, core]
        return remote(ref, ref, ns_s.at[slot], ns_r.at[slot], sibling)

    def start_gather(t, s, first=False):
        if first:
            names_copy(0, True).start()
            names_copy(0, False).start()
        for j in range(2):
            gather_copy(t, s, j, True).start()
            gather_copy(t, s, j, False).start()
        if first:
            names_sibling(1, c).start()
        gather_sibling(t, s, 1, c).start()

    def gather_step(t, s, j):
        for up in (True, False):
            gather_copy(t, s, j, up).wait_recv()
            if j + 2 < UNITS:
                gather_copy(t, s, j + 2, up).start()
        if j % 2 == 1:
            d = j // 2
            for slots in (BELOW, ABOVE):
                gather_sibling(t, s, slots[d + 1], c).start()
        if j == UNITS - 1:
            gather_sibling(t, s, 0, c).start()
        if s == 0 and j % 2 == 1:

            @pl.when(t == 0)
            def _():
                d = j // 2
                for up, slots in ((True, BELOW), (False, ABOVE)):
                    names_copy(d, up).wait_recv()
                    if d + 1 < (4 if up else 3):
                        names_copy(d + 1, up).start()
                    names_sibling(slots[d + 1], c).start()

        if s == 0 and j == UNITS - 1:

            @pl.when(t == 0)
            def _():
                names_copy(3, True).wait_recv()
                names_sibling(0, c).start()

    def finish_gather(t, s):
        for j in range(UNITS):
            gather_copy(t, s, j, True).wait_send()
            gather_copy(t, s, j, False).wait_send()
        for slot in range(SLOTS):
            gather_sibling(t, s, slot, c).wait_send()

    def part_sibling(t, s, slot):
        return remote(
            part.at[t, s, slot, 1 - c],
            sib_part.at[t, s, slot],
            rs_s.at[t, s, slot],
            rs_r.at[t, s, slot],
            sibling,
        )

    def compute(t, s, q):
        pair = pl.ds(2 * q, 2)
        for slot in (2 * q, 2 * q + 1):
            gather_sibling(t, s, slot, 1 - c).wait_recv()
        if s == 0:

            @pl.when(t == 0)
            def _():
                for slot in (2 * q, 2 * q + 1):
                    names_sibling(slot, 1 - c).wait_recv()

        count = 4 * rows
        tokens = held[t, s, pair].reshape(count, width)
        acts = jnp.dot(tokens, both[...], preferred_element_type=jnp.float32)
        gate_act, up_act = acts[:, :units], acts[:, units:]
        lane = lax.broadcasted_iota(jnp.int32, (count, LANES), 1)
        names = named[pair].reshape(count, LANES).astype(jnp.float32)
        name = jnp.sum(jnp.where(lane == 2 * t + s, names, 0.0), axis=1, keepdims=True)
        hidden = gate_act * jax.nn.sigmoid(gate_act) * up_act
        hidden = jnp.where(name == mine, hidden, 0.0).astype(jnp.bfloat16)
        step = 512
        for start in range(0, width, step):
            cols = pl.ds(start, step)
            product = jnp.dot(hidden, down[:, cols], preferred_element_type=jnp.float32)
            part[t, s, pair, :, :, cols] = product.astype(jnp.bfloat16).reshape(2, 2, rows, step)
        for slot in (2 * q, 2 * q + 1):
            part_sibling(t, s, slot).start()

    def reduce_copy(t, s, j, up):
        d, h = (REDUCE_UP if up else REDUCE_DOWN)[j]
        slot = (ABOVE if up else BELOW)[d]
        return remote(
            part.at[t, s, slot, c, half(h)],
            (from_below if up else from_above).at[t, s, d - 1, half(h)],
            (ru_s if up else rd_s).at[t, s, j],
            (ru_r if up else rd_r).at[t, s, j],
            above if up else below,
        )

    def reduce_send(t, s, j, up):
        d, h = (REDUCE_UP if up else REDUCE_DOWN)[j]
        slot = (ABOVE if up else BELOW)[d]
        total = part[t, s, slot, c, half(h)].astype(jnp.float32)
        total = total + sib_part[t, s, slot, half(h)].astype(jnp.float32)
        if j >= 2:
            came = from_below if up else from_above
            total = total + came[t, s, d, half(h)].astype(jnp.float32)
        part[t, s, slot, c, half(h)] = total.astype(jnp.bfloat16)
        reduce_copy(t, s, j, up).start()

    def start_reduce(t, s):
        part_sibling(t, s, 0).wait_recv()
        for up in (True, False):
            reduce_send(t, s, 0, up)
        for up in (True, False):
            part_sibling(t, s, (ABOVE if up else BELOW)[3]).wait_recv()
            reduce_send(t, s, 1, up)

    def reduce_step(t, s, j):
        if j in (1, 3):
            for slots in (ABOVE, BELOW):
                part_sibling(t, s, slots[2 if j == 1 else 1]).wait_recv()
        for up in (True, False):
            reduce_copy(t, s, j, up).wait_recv()
            if j + 2 < UNITS:
                reduce_send(t, s, j + 2, up)

    def finish_reduce(t, s):
        for j in range(UNITS):
            reduce_copy(t, s, j, True).wait_send()
            reduce_copy(t, s, j, False).wait_send()
        for slot in range(SLOTS):
            part_sibling(t, s, slot).wait_send()

    def normalize(t, s):
        route = routes[s][t]
        for h in range(2):
            rows_of = half(h)
            widened = current[s, rows_of].astype(jnp.float32)
            mean = jnp.mean(widened * widened, axis=-1, keepdims=True)
            normed = widened * lax.rsqrt(mean + epsilon) * gains[...]
            normed = normed.astype(jnp.bfloat16)
            held[t, s, 1, c, rows_of] = normed
            chosen = route[h * half_rows : (h + 1) * half_rows]
            column = jnp.where(chosen == 0, router[0:1], router[1:2])
            score = jnp.sum(normed.astype(jnp.float32) * column, axis=1, keepdims=True)
            weight[s, rows_of] = jnp.broadcast_to(
                route_scale * jax.nn.sigmoid(score), (half_rows, LANES)
            )

    def pipe_copy(s):
        return remote(
            outs[s].at[0],
            arrived.at[s],
            pipe_s.at[s],
            pipe_r.at[s],
            onward if s == 0 else backward,
        )

    def receive(s):
        pipe_copy(s).wait_recv()
        current[s] = arrived[s]

        @pl.when(p == (0 if s == 0 else sections - 1))
        def _():
            current[s] = enters[s][0]

    def finalize(t, s):
        part_sibling(t, s, 1).wait_recv()
        for h in range(2):
            rows_of = half(h)
            total = part[t, s, 1, c, rows_of].astype(jnp.float32)
            total = total + sib_part[t, s, 1, rows_of].astype(jnp.float32)
            total = total + from_below[t, s, 0, rows_of].astype(jnp.float32)
            total = total + from_above[t, s, 0, rows_of].astype(jnp.float32)
            widened = current[s, rows_of].astype(jnp.float32)
            result = widened + weight[s, rows_of, 0:1] * total
            outs[s][t, rows_of] = result.astype(jnp.bfloat16)

        @pl.when(t == 0)
        def _():
            pipe_copy(s).start()

    barrier = pltpu.get_barrier_semaphore()
    partners = (above, below, sibling, onward, backward)
    for partner in partners:
        pl.semaphore_signal(barrier, inc=1, device_id=partner, device_id_type=MESH)
    loads = (
        pltpu.make_async_copy(gate_hbm, both.at[:, pl.ds(0, units)], load_sem.at[0]),
        pltpu.make_async_copy(up_hbm, both.at[:, pl.ds(units, units)], load_sem.at[1]),
        pltpu.make_async_copy(down_hbm, down, load_sem.at[2]),
    )
    for load in loads:
        load.start()
    lane = lax.broadcasted_iota(jnp.int32, (rows, LANES), 1)
    own = jnp.zeros((rows, LANES), jnp.float32)
    for step in range(2):
        for s in range(2):
            own = jnp.where(lane == 2 * step + s, routes[s][step].astype(jnp.float32), own)
    named[1, c] = own.astype(jnp.bfloat16)
    current[0] = states[0][0]
    normalize(0, 0)
    pl.semaphore_wait(barrier, len(partners))
    start_gather(0, 0, first=True)
    current[1] = states[1][0]
    normalize(0, 1)
    for load in loads:
        load.wait()

    def one_step(t, carry):
        for j in range(UNITS):
            gather_step(t, 0, j)
            if j == 3:

                @pl.when(t > 0)
                def _():
                    receive(1)
                    normalize(t, 1)

                start_gather(t, 1)
        for j in range(UNITS):
            gather_step(t, 1, j)
            if j < CHUNKS:
                compute(t, 0, j)
            if j == 5:
                start_reduce(t, 0)
        for j in range(UNITS):
            reduce_step(t, 0, j)
            if j < CHUNKS:
                compute(t, 1, j)
            if j == 5:
                start_reduce(t, 1)
        finalize(t, 0)
        for j in range(UNITS):
            reduce_step(t, 1, j)
            if j == 3:

                @pl.when(t == 0)
                def _():
                    receive(0)
                    normalize(1, 0)
                    start_gather(1, 0)

        finalize(t, 1)
        for s in range(2):
            finish_gather(t, s)
            finish_reduce(t, s)
        return carry

    lax.fori_loop(0, 2, one_step, 0)
    for s in range(2):
        pipe_copy(s).wait_send()
    for d in range(4):
        names_copy(d, True).wait_send()
    for d in range(3):
        names_copy(d, False).wait_send()
    for slot in range(SLOTS):
        names_sibling(slot, c).wait_send()


def shards(
    first_state,
    second_state,
    first_enter,
    second_enter,
    norm_gain,
    router,
    gate_proj,
    up_proj,
    down_proj,
    first_routes,
    second_routes,
):
    chips = lax.axis_size("expert") // 2
    sections = lax.axis_size("pipe")
    rows, width = first_state.shape[1:]
    units = gate_proj.shape[2]
    steps = first_routes.shape[0]
    vmem = pl.BlockSpec(memory_space=pltpu.VMEM)
    hbm = pl.BlockSpec(memory_space=pl.ANY)
    bf16 = jnp.bfloat16
    dma = pltpu.SemaphoreType.DMA
    out = jax.ShapeDtypeStruct((steps, rows, width), bf16)
    outs = pl.pallas_call(
        functools.partial(relay_kernel, chips, sections),
        out_shape=(out, out),
        in_specs=[vmem] * 6 + [hbm] * 3 + [vmem] * 2,
        out_specs=(vmem, vmem),
        scratch_shapes=[
            pltpu.VMEM((steps, 2, SLOTS, 2, rows, width), bf16),
            pltpu.VMEM((steps, 2, SLOTS, 2, rows, width), bf16),
            pltpu.VMEM((steps, 2, SLOTS, rows, width), bf16),
            pltpu.VMEM((steps, 2, 4, rows, width), bf16),
            pltpu.VMEM((steps, 2, 4, rows, width), bf16),
            pltpu.VMEM((2, rows, width), bf16),
            pltpu.VMEM((2, rows, width), bf16),
            pltpu.VMEM((2, rows, LANES), jnp.float32),
            pltpu.VMEM((width, 2 * units), bf16),
            pltpu.VMEM((units, width), bf16),
            pltpu.VMEM((SLOTS, 2, rows, LANES), bf16),
        ]
        + [dma((steps, 2, UNITS))] * 4
        + [dma((steps, 2, SLOTS))] * 2
        + [dma((steps, 2, UNITS))] * 4
        + [dma((steps, 2, SLOTS))] * 2
        + [dma((2,))] * 2
        + [dma((4,))] * 4
        + [dma((SLOTS,))] * 2
        + [dma((3,))],
        compiler_params=pltpu.CompilerParams(
            collective_id=0, has_side_effects=True, vmem_limit_bytes=60 << 20
        ),
        name="relay_window",
    )(
        first_state,
        second_state,
        first_enter,
        second_enter,
        norm_gain,
        router[0].T,
        gate_proj[0],
        up_proj[0],
        down_proj[0],
        first_routes[:, 0],
        second_routes[:, 0],
    )
    return (outs[0][:, None], outs[1][:, None])


def solution(mesh):
    return jax.shard_map(
        shards,
        mesh=mesh,
        in_specs=(
            P("pipe", "expert", None),
            P("pipe", "expert", None),
            P(None, "expert", None),
            P(None, "expert", None),
            P("pipe", None),
            P("pipe", None, None),
            P("pipe", None, "expert"),
            P("pipe", None, "expert"),
            P("pipe", "expert", None),
            P(None, "pipe", "expert", None),
            P(None, "pipe", "expert", None),
        ),
        out_specs=(P(None, "pipe", "expert", None), P(None, "pipe", "expert", None)),
        check_vma=False,
    )
```

```python
import functools

import jax
import jax.numpy as jnp
from jax import lax
from jax.experimental import pallas as pl
from jax.experimental.pallas import tpu as pltpu
from jax.sharding import PartitionSpec as P

EXP_WIN = 2
MESH = pl.DeviceIdType.MESH

epsilon = 1e-06
route_scale = 2.5

LANES = 128
FOLD = 256
REACH = 5
PIECES = 2


ORDER = (
    ("prepare", 0, 0),
    ("start", 0, 0),
    ("gather", 0, 0, 1, 0),
    ("prepare", 0, 1),
    ("gather", 0, 0, 1, 1),
    ("start", 0, 1),
    ("gather", 0, 0, 2, 0),
    ("gather", 0, 0, 2, 1),
    ("gather", 0, 1, 1, 0),
    ("gather", 0, 0, 3, 0),
    ("gather", 0, 1, 1, 1),
    ("gather", 0, 0, 3, 1),
    ("gather", 0, 1, 2, 0),
    ("gather", 0, 0, 4, 0),
    ("gather", 0, 0, 4, 1),
    ("gather", 0, 1, 2, 1),
    ("gather", 0, 1, 3, 0),
    ("gather", 0, 0, 5, 0),
    ("gather", 0, 0, 5, 1),
    ("compute", 0, 0),
    ("gather", 0, 1, 3, 1),
    ("total", 0, 0, 5),
    ("gather", 0, 1, 4, 0),
    ("gather", 0, 1, 4, 1),
    ("gather", 0, 1, 5, 0),
    ("total", 0, 0, 4),
    ("reduce", 0, 0, 1, 0),
    ("reduce", 0, 0, 1, 1),
    ("gather", 0, 1, 5, 1),
    ("total", 0, 0, 3),
    ("reduce", 0, 0, 2, 0),
    ("reduce", 0, 0, 2, 1),
    ("compute", 0, 1),
    ("total", 0, 1, 5),
    ("total", 0, 0, 2),
    ("reduce", 0, 0, 3, 0),
    ("reduce", 0, 0, 3, 1),
    ("total", 0, 0, 1),
    ("total", 0, 1, 4),
    ("reduce", 0, 1, 1, 0),
    ("reduce", 0, 0, 4, 0),
    ("reduce", 0, 1, 1, 1),
    ("reduce", 0, 0, 4, 1),
    ("total", 0, 1, 3),
    ("reduce", 0, 1, 2, 0),
    ("reduce", 0, 0, 5, 0),
    ("reduce", 0, 1, 2, 1),
    ("reduce", 0, 0, 5, 1),
    ("finish", 0, 0, 0),
    ("finish", 0, 0, 1),
    ("total", 0, 1, 2),
    ("reduce", 0, 1, 3, 0),
    ("reduce", 0, 1, 3, 1),
    ("total", 0, 1, 1),
    ("reduce", 0, 1, 4, 0),
    ("reduce", 0, 1, 4, 1),
    ("prepare", 1, 0),
    ("reduce", 0, 1, 5, 0),
    ("reduce", 0, 1, 5, 1),
    ("finish", 0, 1, 0),
    ("start", 1, 0),
    ("finish", 0, 1, 1),
    ("gather", 1, 0, 1, 0),
    ("gather", 1, 0, 1, 1),
    ("gather", 1, 0, 2, 0),
    ("prepare", 1, 1),
    ("gather", 1, 0, 2, 1),
    ("start", 1, 1),
    ("gather", 1, 0, 3, 0),
    ("gather", 1, 1, 1, 0),
    ("gather", 1, 1, 1, 1),
    ("gather", 1, 0, 3, 1),
    ("gather", 1, 1, 2, 0),
    ("gather", 1, 0, 4, 0),
    ("gather", 1, 0, 4, 1),
    ("gather", 1, 1, 2, 1),
    ("gather", 1, 0, 5, 0),
    ("gather", 1, 0, 5, 1),
    ("compute", 1, 0),
    ("total", 1, 0, 5),
    ("gather", 1, 1, 3, 0),
    ("total", 1, 0, 4),
    ("gather", 1, 1, 3, 1),
    ("gather", 1, 1, 4, 0),
    ("gather", 1, 1, 4, 1),
    ("gather", 1, 1, 5, 0),
    ("reduce", 1, 0, 1, 0),
    ("reduce", 1, 0, 1, 1),
    ("total", 1, 0, 3),
    ("gather", 1, 1, 5, 1),
    ("compute", 1, 1),
    ("total", 1, 1, 5),
    ("reduce", 1, 0, 2, 0),
    ("total", 1, 1, 4),
    ("reduce", 1, 0, 2, 1),
    ("reduce", 1, 1, 1, 0),
    ("reduce", 1, 1, 1, 1),
    ("total", 1, 0, 2),
    ("total", 1, 1, 3),
    ("reduce", 1, 0, 3, 0),
    ("reduce", 1, 1, 2, 0),
    ("reduce", 1, 1, 2, 1),
    ("reduce", 1, 0, 3, 1),
    ("total", 1, 1, 2),
    ("total", 1, 0, 1),
    ("reduce", 1, 1, 3, 0),
    ("reduce", 1, 1, 3, 1),
    ("reduce", 1, 0, 4, 0),
    ("total", 1, 1, 1),
    ("reduce", 1, 1, 4, 0),
    ("reduce", 1, 1, 4, 1),
    ("reduce", 1, 0, 4, 1),
    ("reduce", 1, 0, 5, 0),
    ("reduce", 1, 1, 5, 0),
    ("reduce", 1, 1, 5, 1),
    ("finish", 1, 1, 0),
    ("reduce", 1, 0, 5, 1),
    ("finish", 1, 1, 1),
    ("finish", 1, 0, 0),
    ("finish", 1, 0, 1),
)


def relay_kernel(
    chips,
    sections,
    first_state,
    second_state,
    first_enter,
    second_enter,
    gains,
    router,
    gate_hbm,
    up_hbm,
    down_hbm,
    first_routes,
    second_routes,
    first_out,
    second_out,
    held,
    other,
    part,
    sums,
    other_sum,
    arrived,
    current,
    weight,
    both,
    down,
    fold,
    outcome,
    extra_in,
    extra_out,
    fold_sum,
    g_s,
    g_r,
    r_s,
    r_r,
    share_s,
    share_r,
    pipe_s,
    pipe_r,
    load_sem,
):
    rows, width = current.shape[1:]
    half_rows = rows // 2
    units = gate_hbm.shape[1]
    folds = width // LANES
    piece = (width + FOLD) // PIECES
    group = chips // EXP_WIN
    e = lax.axis_index("expert")
    p = lax.axis_index("pipe")
    z, c = e // 2, e % 2
    own_expert = (z // group).astype(jnp.float32)
    above = {"expert": ((z + 1) % chips) * 2 + c}
    below = {"expert": ((z + chips - 1) % chips) * 2 + c}
    sibling = {"expert": z * 2 + (1 - c)}
    further = (
        {"expert": ((z + chips - 2) % chips) * 2 + c},
        {"expert": ((z + 2) % chips) * 2 + c},
    )
    onward = {"pipe": (p + 1) % sections}
    backward = {"pipe": (p + sections - 1) % sections}
    nexts = (below, above)
    ranks = (z % group, group - 1 - z % group)
    routes = (first_routes, second_routes)
    states = (first_state, second_state)
    enters = (first_enter, second_enter)
    outs = (first_out, second_out)

    def ahead(way, distance):
        return (z + (chips - distance if way == 0 else distance)) % chips

    def behind(way, distance):
        return ahead(1 - way, distance)

    def remote(src, dst, send, recv, device):
        return pltpu.make_async_remote_copy(
            src_ref=src,
            dst_ref=dst,
            send_sem=send,
            recv_sem=recv,
            device_id=device,
            device_id_type=MESH,
        )

    def columns(h):
        return pl.ds(h * piece, piece)

    def gather_copy(t, s, way, src, chip, index, h, device):
        return remote(
            src.at[:, columns(h)],
            held.at[t, s, chip, :, columns(h)],
            g_s.at[way, t, s, index, h],
            g_r.at[way, t, s, index, h],
            device,
        )

    def gather_own(t, s, way, h):
        return gather_copy(t, s, way, held.at[t, s, z], z, 1, h, nexts[way])

    def gather_other(t, s, way, h):
        return gather_copy(t, s, way, other.at[t, s], z, 1, h, nexts[way])

    def gather_further(t, s, way, h):
        return gather_copy(t, s, way, other.at[t, s], z, 2, h, further[way])

    def gather_forward(t, s, way, d, h):
        chip = behind(way, d)
        return gather_copy(t, s, way, held.at[t, s, chip], chip, d + 1, h, nexts[way])

    def gather_arrival(t, s, way, d, h):
        chip = behind(way, d)
        return gather_copy(t, s, way, held.at[t, s, chip], chip, d, h, nexts[way])

    def start_gather(t, s):
        for h in range(PIECES):
            for way, rank in enumerate(ranks):

                @pl.when(rank == 1)
                def _():
                    gather_further(t, s, way, h).start()

                @pl.when(rank == 0)
                def _():
                    gather_other(t, s, way, h).start()

                @pl.when(rank >= 1)
                def _():
                    gather_own(t, s, way, h).start()

    def gather_step(t, s, d, h):
        for way, rank in enumerate(ranks):

            @pl.when(rank <= REACH - d)
            def _():
                gather_arrival(t, s, way, d, h).wait_recv()
                if d < REACH:

                    @pl.when(rank >= 1)
                    def _():
                        gather_forward(t, s, way, d, h).start()

    def finish_gather(t, s):
        for h in range(PIECES):
            for way, rank in enumerate(ranks):

                @pl.when(rank == 1)
                def _():
                    gather_further(t, s, way, h).wait_send()

                @pl.when(rank == 0)
                def _():
                    gather_other(t, s, way, h).wait_send()

                @pl.when(rank >= 1)
                def _():
                    gather_own(t, s, way, h).wait_send()

                for d in range(1, REACH):

                    @pl.when((rank <= REACH - d) & (rank >= 1))
                    def _():
                        gather_forward(t, s, way, d, h).wait_send()

    def share_copies():
        own, theirs = pl.ds(0, units), pl.ds(units, units)
        targets = (
            (gate_hbm, both.at[:, theirs]),
            (up_hbm, both.at[:, pl.ds(3 * units, units)]),
            (down_hbm, down.at[theirs]),
        )
        return [
            remote(src, dst, share_s.at[i], share_r.at[i], sibling)
            for i, (src, dst) in enumerate(targets)
        ]

    def place(k):
        return (k % half_rows), pl.ds((k // half_rows) * LANES, LANES)

    def compute(t, s):
        count = chips * half_rows
        along = lax.broadcasted_iota(jnp.int32, (count, count), 0)
        across = lax.broadcasted_iota(jnp.int32, (count, count), 1)

        def turning(inner, outer):
            onehot = across == (along % outer) * inner + along // outer
            return onehot.astype(jnp.float32).astype(jnp.bfloat16)

        folded = held[t, s, :, :, 0:FOLD].reshape(count, FOLD)
        turned = jnp.dot(
            turning(half_rows, chips), folded, preferred_element_type=jnp.float32
        )
        for k in range(folds):
            row, lanes = place(k)
            start = (k // half_rows) * LANES
            extra_in[0:chips, k * LANES : (k + 1) * LANES] = turned[
                row * chips : (row + 1) * chips, start : start + LANES
            ]
        tokens = held[t, s, :, :, FOLD : FOLD + width].reshape(count, width)
        tokens = jnp.concatenate([tokens, extra_in[...].astype(jnp.bfloat16)], axis=0)
        acts = jnp.dot(tokens, both[...], preferred_element_type=jnp.float32)
        gate_act, up_act = acts[:, : 2 * units], acts[:, 2 * units :]
        hidden = (gate_act * jax.nn.sigmoid(gate_act) * up_act).astype(jnp.bfloat16)
        step = 2 * LANES
        for start in range(0, width, step):
            product = jnp.dot(
                hidden, down[:, pl.ds(start, step)], preferred_element_type=jnp.float32
            )
            for k in range(start // LANES, (start + step) // LANES):
                row, lanes = place(k)
                at = k * LANES - start
                extra_out[row * chips : (row + 1) * chips, lanes] = product[
                    count : count + chips, at : at + LANES
                ]
            product = product[:count].astype(jnp.bfloat16).reshape(chips, half_rows, step)
            part[t, s, :, :, pl.ds(FOLD + start, step)] = product
        folded = jnp.dot(
            turning(chips, half_rows),
            extra_out[...].astype(jnp.bfloat16),
            preferred_element_type=jnp.float32,
        )
        part[t, s, :, :, 0:FOLD] = folded.astype(jnp.bfloat16).reshape(chips, half_rows, FOLD)

    def reduce_copy(t, s, way, d, h, dst, index, device):
        return remote(
            part.at[t, s, ahead(way, d), :, columns(h)],
            dst.at[:, columns(h)],
            r_s.at[way, t, s, index, h],
            r_r.at[way, t, s, index, h],
            device,
        )

    def reduce_on(t, s, way, d, h):
        return reduce_copy(t, s, way, d, h, sums.at[way, t, s, d - 1], d - 1, nexts[way])

    def reduce_out(t, s, way, d, h):
        device = nexts[way] if d == 1 else further[way]
        return reduce_copy(t, s, way, d, h, other_sum.at[t, s], REACH, device)

    def add_up(t, s, way, d, h):
        home, cols = ahead(way, d), columns(h)
        total = part[t, s, home, :, cols].astype(jnp.float32)
        total = total + sums[way, t, s, d, :, cols].astype(jnp.float32)
        part[t, s, home, :, cols] = total.astype(jnp.bfloat16)

    def start_reduce(t, s, d):
        for way, rank in enumerate(ranks):

            @pl.when(rank == group - 1)
            def _():
                for h in range(PIECES):
                    reduce_on(t, s, way, d, h).start()

    def reduce_step(t, s, r, h):
        d = REACH - r
        for way, rank in enumerate(ranks):

            @pl.when((rank >= d - 2) & (rank < group - 1))
            def _():
                reduce_on(t, s, way, d + 1, h).wait_recv()
                if d >= 1:
                    add_up(t, s, way, d, h)

                    @pl.when(rank >= 1)
                    def _():
                        reduce_on(t, s, way, d, h).start()

                    if d <= 2:

                        @pl.when(rank == 0)
                        def _():
                            reduce_out(t, s, way, d, h).start()

            if d == 0:

                @pl.when(rank >= group - 2)
                def _():
                    reduce_out(t, s, way, 1, h).wait_recv()

    def finish_reduce(t, s):
        for h in range(PIECES):
            for way, rank in enumerate(ranks):

                @pl.when(rank == group - 1)
                def _():
                    for d in range(REACH, 0, -1):
                        reduce_on(t, s, way, d, h).wait_send()

                for d in range(1, REACH):

                    @pl.when((rank >= d - 2) & (rank < group - 1) & (rank >= 1))
                    def _():
                        reduce_on(t, s, way, d, h).wait_send()

                @pl.when(rank == 0)
                def _():
                    reduce_out(t, s, way, 2, h).wait_send()
                    reduce_out(t, s, way, 1, h).wait_send()

    def packing(t, s):
        along = lax.broadcasted_iota(jnp.int32, (rows, rows), 0)
        across = lax.broadcasted_iota(jnp.int32, (rows, rows), 1)

        def column(row):
            spread = jnp.broadcast_to(row, (rows, rows))
            return jnp.sum(jnp.where(across == along, spread, 0.0), axis=1, keepdims=True)

        named = routes[s][t].astype(jnp.float32)
        away = jnp.abs(named - own_expert)
        before = jnp.where(along < across, jnp.broadcast_to(column(away), (rows, rows)), 0.0)
        before = jnp.sum(before, axis=0, keepdims=True)
        index = lax.broadcasted_iota(jnp.int32, (1, rows), 1).astype(jnp.float32)
        order = jnp.where(away > 0.5, before, index - before)
        spare = jnp.where(away > 0.5, half_rows - 1.0, rows - 1.0)
        put = jnp.where(order < half_rows, order + half_rows * away, spare)
        return along, across, named, put, column(put), jnp.sum(away, axis=1, keepdims=True)

    def prepare(t, s):
        along, across, named, put, _, _ = packing(t, s)
        onehot = (along.astype(jnp.float32) == put).astype(jnp.float32)
        chosen = jnp.sum(onehot * named, axis=1, keepdims=True)
        packed = jnp.dot(
            onehot.astype(jnp.bfloat16), current[s], preferred_element_type=jnp.float32
        )
        current[s] = packed.astype(jnp.bfloat16)
        for h in range(2):
            widened = packed[h * half_rows : (h + 1) * half_rows]
            mean = jnp.mean(widened * widened, axis=-1, keepdims=True)
            normed = widened * lax.rsqrt(mean + epsilon) * gains[...]
            normed = normed.astype(jnp.bfloat16)
            if h == 0:
                held[t, s, z, :, FOLD : FOLD + width] = normed
            else:
                other[t, s, :, FOLD : FOLD + width] = normed
            normed = normed.astype(jnp.float32)
            for k in range(folds):
                row, lanes = place(k)
                fold[1 - h, row : row + 1, lanes] = normed[
                    half_rows - 1 : half_rows, k * LANES : (k + 1) * LANES
                ]
            part_of = chosen[h * half_rows : (h + 1) * half_rows]
            column = jnp.where(part_of < 0.5, router[0:1], router[1:2])
            score = jnp.sum(normed * column, axis=1, keepdims=True)
            weight[s, h * half_rows : (h + 1) * half_rows] = jnp.broadcast_to(
                route_scale * jax.nn.sigmoid(score), (half_rows, LANES)
            )
        held[t, s, z, :, 0:FOLD] = fold[0].astype(jnp.bfloat16)
        other[t, s, :, 0:FOLD] = fold[1].astype(jnp.bfloat16)

    def main_columns(h):
        first = max(h * piece, FOLD) - FOLD
        return first, (h + 1) * piece - FOLD

    def pipe_copy(s, h):
        first, last = main_columns(h)
        cols = pl.ds(first, last - first)
        return remote(
            outs[s].at[0, :, cols],
            arrived.at[s, :, cols],
            pipe_s.at[s, h],
            pipe_r.at[s, h],
            onward if s == 0 else backward,
        )

    def receive(s):
        for h in range(PIECES):
            pipe_copy(s, h).wait_recv()
        current[s] = arrived[s]

        @pl.when(p == (0 if s == 0 else sections - 1))
        def _():
            current[s] = enters[s][0]

    def finalize(t, s, h):
        _, across, _, _, put, load = packing(t, s)
        first, last = main_columns(h)

        def sums_of(cols):
            total = part[t, s, z, :, cols].astype(jnp.float32)
            total = total + sums[0, t, s, 0, :, cols].astype(jnp.float32)
            total = total + sums[1, t, s, 0, :, cols].astype(jnp.float32)
            return total, other_sum[t, s, :, cols].astype(jnp.float32)

        if h == 0:
            fold_sum[0], fold_sum[1] = sums_of(pl.ds(0, FOLD))
        crowded = (load > half_rows + 0.5, load < half_rows - 0.5)
        both_sums = sums_of(pl.ds(FOLD + first, last - first))
        for b in range(2):
            outcome[b * half_rows : (b + 1) * half_rows, first:last] = both_sums[b]
            end = (b + 1) * half_rows - 1
            for k in range(first // LANES, last // LANES):
                row, lanes = place(k)
                here = pl.ds(k * LANES, LANES)
                outcome[end : end + 1, here] = jnp.where(
                    crowded[b], fold_sum[1 - b, row : row + 1, lanes], outcome[end : end + 1, here]
                )
        widened = current[s, :, first:last].astype(jnp.float32)
        result = widened + weight[s, :, 0:1] * outcome[:, first:last]
        back = (across.astype(jnp.float32) == put).astype(jnp.float32).astype(jnp.bfloat16)
        result = jnp.dot(back, result.astype(jnp.bfloat16), preferred_element_type=jnp.float32)
        outs[s][t, :, first:last] = result.astype(jnp.bfloat16)
        if t == 0:
            pipe_copy(s, h).start()

    barrier = pltpu.get_barrier_semaphore()
    partners = (above, below, sibling, onward, backward) + further
    for partner in partners:
        pl.semaphore_signal(barrier, inc=1, device_id=partner, device_id_type=MESH)
    loads = (
        pltpu.make_async_copy(gate_hbm, both.at[:, pl.ds(0, units)], load_sem.at[0]),
        pltpu.make_async_copy(up_hbm, both.at[:, pl.ds(2 * units, units)], load_sem.at[1]),
        pltpu.make_async_copy(down_hbm, down.at[pl.ds(0, units)], load_sem.at[2]),
    )
    for load in loads:
        load.start()
    fold[...] = jnp.zeros_like(fold)
    extra_in[...] = jnp.zeros_like(extra_in)
    extra_out[...] = jnp.zeros_like(extra_out)
    for way, rank in enumerate(ranks):

        @pl.when(rank == group - 1)
        def _():
            for t in range(2):
                for s in range(2):
                    sums[way, t, s, 0] = jnp.zeros_like(sums[way, t, s, 0])

    entered = []
    for step, t, s, *at in ORDER:
        if step == "prepare":
            if t == 0:
                current[s] = states[s][0]
            else:
                receive(s)
            prepare(t, s)
        elif step == "start":
            if not entered:
                pl.semaphore_wait(barrier, len(partners))
            start_gather(t, s)
            if not entered:
                for copy in share_copies():
                    copy.start()
            entered.append(step)
        elif step == "gather":
            gather_step(t, s, *at)
        elif step == "compute":
            if (t, s) == (0, 0):
                for load in loads:
                    load.wait()
                for copy in share_copies():
                    copy.wait()
            compute(t, s)
        elif step == "total":
            start_reduce(t, s, *at)
        elif step == "reduce":
            reduce_step(t, s, *at)
        else:
            finalize(t, s, *at)
    for s in range(2):
        for t in range(2):
            finish_gather(t, s)
            finish_reduce(t, s)
        for h in range(PIECES):
            pipe_copy(s, h).wait_send()


def shards(
    first_state,
    second_state,
    first_enter,
    second_enter,
    norm_gain,
    router,
    gate_proj,
    up_proj,
    down_proj,
    first_routes,
    second_routes,
):
    chips = lax.axis_size("expert") // 2
    sections = lax.axis_size("pipe")
    rows, width = first_state.shape[1:]
    half_rows, across = rows // 2, width + FOLD
    units = gate_proj.shape[2]
    steps = first_routes.shape[0]
    vmem = pl.BlockSpec(memory_space=pltpu.VMEM)
    hbm = pl.BlockSpec(memory_space=pl.ANY)
    bf16 = jnp.bfloat16
    dma = pltpu.SemaphoreType.DMA
    out = jax.ShapeDtypeStruct((steps, rows, width), bf16)
    outs = pl.pallas_call(
        functools.partial(relay_kernel, chips, sections),
        out_shape=(out, out),
        in_specs=[vmem] * 6 + [hbm] * 3 + [vmem] * 2,
        out_specs=(vmem, vmem),
        scratch_shapes=[
            pltpu.VMEM((steps, 2, chips, half_rows, across), bf16),
            pltpu.VMEM((steps, 2, half_rows, across), bf16),
            pltpu.VMEM((steps, 2, chips, half_rows, across), bf16),
            pltpu.VMEM((2, steps, 2, REACH, half_rows, across), bf16),
            pltpu.VMEM((steps, 2, half_rows, across), bf16),
            pltpu.VMEM((2, rows, width), bf16),
            pltpu.VMEM((2, rows, width), bf16),
            pltpu.VMEM((2, rows, LANES), jnp.float32),
            pltpu.VMEM((width, 4 * units), bf16),
            pltpu.VMEM((2 * units, width), bf16),
            pltpu.VMEM((2, half_rows, FOLD), jnp.float32),
            pltpu.VMEM((rows, width), jnp.float32),
            pltpu.VMEM((2 * chips, width), jnp.float32),
            pltpu.VMEM((chips * half_rows, FOLD), jnp.float32),
            pltpu.VMEM((2, half_rows, FOLD), jnp.float32),
        ]
        + [dma((2, steps, 2, REACH + 1, PIECES))] * 4
        + [dma((3,))] * 2
        + [dma((2, PIECES))] * 2
        + [dma((3,))],
        compiler_params=pltpu.CompilerParams(
            collective_id=0, has_side_effects=True, vmem_limit_bytes=60 << 20
        ),
        name="relay_window",
    )(
        first_state,
        second_state,
        first_enter,
        second_enter,
        norm_gain,
        router[0].T,
        gate_proj[0],
        up_proj[0],
        down_proj[0],
        first_routes.reshape(steps, 1, rows),
        second_routes.reshape(steps, 1, rows),
    )
    return (outs[0][:, None], outs[1][:, None])


def solution(mesh):
    return jax.shard_map(
        shards,
        mesh=mesh,
        in_specs=(
            P("pipe", "expert", None),
            P("pipe", "expert", None),
            P(None, "expert", None),
            P(None, "expert", None),
            P("pipe", None),
            P("pipe", None, None),
            P("pipe", None, "expert"),
            P("pipe", None, "expert"),
            P("pipe", "expert", None),
            P(None, "pipe", "expert", None),
            P(None, "pipe", "expert", None),
        ),
        out_specs=(P(None, "pipe", "expert", None), P(None, "pipe", "expert", None)),
        check_vma=False,
    )
```

```python
import functools

import jax
import jax.numpy as jnp
from jax import lax
from jax.experimental import pallas as pl
from jax.experimental.pallas import tpu as pltpu
from jax.sharding import PartitionSpec as P

EXP_WIN = 2
MESH = pl.DeviceIdType.MESH

epsilon = 1e-06
route_scale = 2.5

LANES = 128
FOLD = 256
REACH = 5
PIECES = 2
BATCHES = ((-2, -1, 0, 1, 2), (3, 4, 5))


PREPARE, START, GATHER, COMPUTE, TOTAL, REDUCE, OUTSIDE, SENT, FINISH = range(9)

ORDER = (
    (PREPARE, 0, 0),
    (START, 0, 0),
    (PREPARE, 0, 1),
    (GATHER, 0, 0, 1, 0),
    (GATHER, 0, 0, 1, 1),
    (START, 0, 1),
    (GATHER, 0, 0, 2, 0),
    (GATHER, 0, 0, 2, 1),
    (GATHER, 0, 1, 1, 0),
    (COMPUTE, 0, 0, 0),
    (GATHER, 0, 1, 1, 1),
    (TOTAL, 0, 0, 1),
    (TOTAL, 0, 0, 2),
    (GATHER, 0, 0, 3, 0),
    (GATHER, 0, 0, 3, 1),
    (GATHER, 0, 1, 2, 0),
    (GATHER, 0, 1, 2, 1),
    (REDUCE, 0, 0, 1, 1, 0),
    (COMPUTE, 0, 1, 0),
    (REDUCE, 0, 0, 1, 1, 1),
    (REDUCE, 0, 0, 2, 1, 0),
    (TOTAL, 0, 1, 1),
    (REDUCE, 0, 0, 2, 1, 1),
    (TOTAL, 0, 1, 2),
    (GATHER, 0, 0, 4, 0),
    (GATHER, 0, 0, 4, 1),
    (GATHER, 0, 1, 3, 0),
    (GATHER, 0, 1, 3, 1),
    (REDUCE, 0, 0, 2, 2, 0),
    (REDUCE, 0, 1, 1, 1, 0),
    (REDUCE, 0, 1, 1, 1, 1),
    (REDUCE, 0, 1, 2, 1, 0),
    (REDUCE, 0, 0, 2, 2, 1),
    (GATHER, 0, 0, 5, 0),
    (GATHER, 0, 0, 5, 1),
    (REDUCE, 0, 1, 2, 1, 1),
    (COMPUTE, 0, 0, 1),
    (TOTAL, 0, 0, 5),
    (TOTAL, 0, 0, 4),
    (GATHER, 0, 1, 4, 0),
    (GATHER, 0, 1, 4, 1),
    (REDUCE, 0, 1, 2, 2, 0),
    (SENT, 0, 0, GATHER),
    (REDUCE, 0, 0, 5, 1, 0),
    (REDUCE, 0, 0, 5, 1, 1),
    (TOTAL, 0, 0, 3),
    (REDUCE, 0, 1, 2, 2, 1),
    (GATHER, 0, 1, 5, 0),
    (GATHER, 0, 1, 5, 1),
    (COMPUTE, 0, 1, 1),
    (REDUCE, 0, 0, 4, 1, 0),
    (REDUCE, 0, 0, 4, 1, 1),
    (TOTAL, 0, 1, 5),
    (REDUCE, 0, 0, 5, 2, 0),
    (REDUCE, 0, 0, 5, 2, 1),
    (REDUCE, 0, 0, 3, 1, 0),
    (TOTAL, 0, 1, 4),
    (REDUCE, 0, 0, 3, 1, 1),
    (REDUCE, 0, 0, 4, 2, 0),
    (REDUCE, 0, 0, 4, 2, 1),
    (SENT, 0, 1, GATHER),
    (REDUCE, 0, 1, 5, 1, 0),
    (REDUCE, 0, 0, 5, 3, 0),
    (REDUCE, 0, 1, 5, 1, 1),
    (REDUCE, 0, 0, 5, 3, 1),
    (TOTAL, 0, 1, 3),
    (REDUCE, 0, 0, 3, 2, 0),
    (REDUCE, 0, 0, 3, 2, 1),
    (REDUCE, 0, 1, 4, 1, 0),
    (REDUCE, 0, 0, 4, 3, 0),
    (REDUCE, 0, 0, 4, 3, 1),
    (REDUCE, 0, 0, 3, 3, 0),
    (REDUCE, 0, 1, 4, 1, 1),
    (REDUCE, 0, 1, 5, 2, 0),
    (REDUCE, 0, 1, 5, 2, 1),
    (REDUCE, 0, 0, 3, 3, 1),
    (OUTSIDE, 0, 0, 0),
    (OUTSIDE, 0, 0, 1),
    (FINISH, 0, 0, 0),
    (REDUCE, 0, 1, 3, 1, 0),
    (REDUCE, 0, 1, 3, 1, 1),
    (REDUCE, 0, 1, 4, 2, 0),
    (REDUCE, 0, 1, 4, 2, 1),
    (FINISH, 0, 0, 1),
    (REDUCE, 0, 1, 5, 3, 0),
    (REDUCE, 0, 1, 5, 3, 1),
    (REDUCE, 0, 1, 3, 2, 0),
    (REDUCE, 0, 1, 3, 2, 1),
    (REDUCE, 0, 1, 4, 3, 0),
    (REDUCE, 0, 1, 4, 3, 1),
    (PREPARE, 1, 0),
    (REDUCE, 0, 1, 3, 3, 0),
    (REDUCE, 0, 1, 3, 3, 1),
    (OUTSIDE, 0, 1, 0),
    (OUTSIDE, 0, 1, 1),
    (FINISH, 0, 1, 0),
    (START, 1, 0),
    (FINISH, 0, 1, 1),
    (GATHER, 1, 0, 1, 0),
    (GATHER, 1, 0, 1, 1),
    (PREPARE, 1, 1),
    (START, 1, 1),
    (GATHER, 1, 0, 2, 0),
    (GATHER, 1, 0, 2, 1),
    (COMPUTE, 1, 0, 0),
    (GATHER, 1, 1, 1, 0),
    (GATHER, 1, 1, 1, 1),
    (TOTAL, 1, 0, 1),
    (TOTAL, 1, 0, 2),
    (GATHER, 1, 1, 2, 0),
    (GATHER, 1, 1, 2, 1),
    (SENT, 0, 0, REDUCE),
    (GATHER, 1, 0, 3, 0),
    (GATHER, 1, 0, 3, 1),
    (REDUCE, 1, 0, 1, 1, 0),
    (REDUCE, 1, 0, 1, 1, 1),
    (REDUCE, 1, 0, 2, 1, 0),
    (COMPUTE, 1, 1, 0),
    (TOTAL, 1, 1, 1),
    (TOTAL, 1, 1, 2),
    (SENT, 0, 1, REDUCE),
    (GATHER, 1, 1, 3, 0),
    (GATHER, 1, 1, 3, 1),
    (REDUCE, 1, 0, 2, 1, 1),
    (REDUCE, 1, 1, 1, 1, 0),
    (GATHER, 1, 0, 4, 0),
    (REDUCE, 1, 1, 1, 1, 1),
    (GATHER, 1, 0, 4, 1),
    (REDUCE, 1, 0, 2, 2, 0),
    (REDUCE, 1, 1, 2, 1, 0),
    (REDUCE, 1, 1, 2, 1, 1),
    (GATHER, 1, 1, 4, 0),
    (GATHER, 1, 1, 4, 1),
    (REDUCE, 1, 0, 2, 2, 1),
    (GATHER, 1, 0, 5, 0),
    (GATHER, 1, 0, 5, 1),
    (COMPUTE, 1, 0, 1),
    (TOTAL, 1, 0, 5),
    (TOTAL, 1, 0, 4),
    (REDUCE, 1, 1, 2, 2, 0),
    (REDUCE, 1, 1, 2, 2, 1),
    (GATHER, 1, 1, 5, 0),
    (SENT, 1, 0, GATHER),
    (REDUCE, 1, 0, 5, 1, 0),
    (GATHER, 1, 1, 5, 1),
    (REDUCE, 1, 0, 5, 1, 1),
    (COMPUTE, 1, 1, 1),
    (TOTAL, 1, 1, 5),
    (TOTAL, 1, 1, 4),
    (TOTAL, 1, 0, 3),
    (SENT, 1, 1, GATHER),
    (REDUCE, 1, 1, 5, 1, 0),
    (REDUCE, 1, 1, 5, 1, 1),
    (TOTAL, 1, 1, 3),
    (REDUCE, 1, 0, 4, 1, 0),
    (REDUCE, 1, 0, 4, 1, 1),
    (REDUCE, 1, 1, 4, 1, 0),
    (REDUCE, 1, 1, 4, 1, 1),
    (REDUCE, 1, 0, 5, 2, 0),
    (REDUCE, 1, 0, 5, 2, 1),
    (REDUCE, 1, 0, 3, 1, 0),
    (REDUCE, 1, 1, 5, 2, 0),
    (REDUCE, 1, 1, 5, 2, 1),
    (REDUCE, 1, 0, 3, 1, 1),
    (REDUCE, 1, 0, 4, 2, 0),
    (REDUCE, 1, 0, 4, 2, 1),
    (REDUCE, 1, 1, 3, 1, 0),
    (REDUCE, 1, 1, 3, 1, 1),
    (REDUCE, 1, 1, 4, 2, 0),
    (REDUCE, 1, 0, 5, 3, 0),
    (REDUCE, 1, 1, 4, 2, 1),
    (REDUCE, 1, 0, 5, 3, 1),
    (REDUCE, 1, 0, 3, 2, 0),
    (REDUCE, 1, 1, 5, 3, 0),
    (REDUCE, 1, 0, 3, 2, 1),
    (REDUCE, 1, 1, 5, 3, 1),
    (REDUCE, 1, 1, 3, 2, 0),
    (REDUCE, 1, 1, 3, 2, 1),
    (REDUCE, 1, 0, 4, 3, 0),
    (REDUCE, 1, 0, 4, 3, 1),
    (REDUCE, 1, 1, 4, 3, 0),
    (REDUCE, 1, 1, 4, 3, 1),
    (REDUCE, 1, 0, 3, 3, 0),
    (REDUCE, 1, 0, 3, 3, 1),
    (OUTSIDE, 1, 0, 0),
    (OUTSIDE, 1, 0, 1),
    (REDUCE, 1, 1, 3, 3, 0),
    (FINISH, 1, 0, 0),
    (FINISH, 1, 0, 1),
    (REDUCE, 1, 1, 3, 3, 1),
    (SENT, 1, 0, REDUCE),
    (OUTSIDE, 1, 1, 0),
    (OUTSIDE, 1, 1, 1),
    (FINISH, 1, 1, 0),
    (FINISH, 1, 1, 1),
)


def relay_kernel(
    chips,
    sections,
    first_state,
    second_state,
    first_enter,
    second_enter,
    gains,
    router,
    gate_hbm,
    up_hbm,
    down_hbm,
    first_routes,
    second_routes,
    first_out,
    second_out,
    held,
    other,
    part,
    sums,
    other_sum,
    arrived,
    current,
    weight,
    both,
    down,
    fold,
    outcome,
    extra_in,
    extra_out,
    fold_sum,
    g_s,
    g_r,
    r_s,
    r_r,
    share_s,
    share_r,
    pipe_s,
    pipe_r,
    load_sem,
):
    rows, width = current.shape[1:]
    half_rows = rows // 2
    units = gate_hbm.shape[1]
    folds = width // LANES
    piece = (width + FOLD) // PIECES
    group = chips // EXP_WIN
    e = lax.axis_index("expert")
    p = lax.axis_index("pipe")
    z, c = e // 2, e % 2
    own_expert = (z // group).astype(jnp.float32)
    above = {"expert": ((z + 1) % chips) * 2 + c}
    below = {"expert": ((z + chips - 1) % chips) * 2 + c}
    sibling = {"expert": z * 2 + (1 - c)}
    further = (
        {"expert": ((z + chips - 2) % chips) * 2 + c},
        {"expert": ((z + 2) % chips) * 2 + c},
    )
    onward = {"pipe": (p + 1) % sections}
    backward = {"pipe": (p + sections - 1) % sections}
    nexts = (below, above)
    ranks = (z % group, group - 1 - z % group)
    routes = (first_routes, second_routes)
    states = (first_state, second_state)
    enters = (first_enter, second_enter)
    outs = (first_out, second_out)

    def ahead(way, distance):
        return (z + (chips - distance if way == 0 else distance)) % chips

    def behind(way, distance):
        return ahead(1 - way, distance)

    def remote(src, dst, send, recv, device):
        return pltpu.make_async_remote_copy(
            src_ref=src,
            dst_ref=dst,
            send_sem=send,
            recv_sem=recv,
            device_id=device,
            device_id_type=MESH,
        )

    def columns(h):
        return pl.ds(h * piece, piece)

    def gather_copy(t, s, way, src, chip, index, h, device):
        return remote(
            src.at[:, columns(h)],
            held.at[t, s, chip, :, columns(h)],
            g_s.at[way, t, s, index, h],
            g_r.at[way, t, s, index, h],
            device,
        )

    def gather_own(t, s, way, h):
        return gather_copy(t, s, way, held.at[t, s, z], z, 1, h, nexts[way])

    def gather_other(t, s, way, h):
        return gather_copy(t, s, way, other.at[t, s], z, 1, h, nexts[way])

    def gather_further(t, s, way, h):
        return gather_copy(t, s, way, other.at[t, s], z, 2, h, further[way])

    def gather_forward(t, s, way, d, h):
        chip = behind(way, d)
        return gather_copy(t, s, way, held.at[t, s, chip], chip, d + 1, h, nexts[way])

    def gather_arrival(t, s, way, d, h):
        chip = behind(way, d)
        return gather_copy(t, s, way, held.at[t, s, chip], chip, d, h, nexts[way])

    def start_gather(t, s):
        for h in range(PIECES):
            for way, rank in enumerate(ranks):

                @pl.when(rank == 1)
                def _():
                    gather_further(t, s, way, h).start()

                @pl.when(rank == 0)
                def _():
                    gather_other(t, s, way, h).start()

                @pl.when(rank >= 1)
                def _():
                    gather_own(t, s, way, h).start()

    def gather_step(t, s, d, h):
        for way, rank in enumerate(ranks):

            @pl.when(rank <= REACH - d)
            def _():
                gather_arrival(t, s, way, d, h).wait_recv()
                if d < REACH:

                    @pl.when(rank >= 1)
                    def _():
                        gather_forward(t, s, way, d, h).start()

    def finish_gather(t, s):
        for h in range(PIECES):
            for way, rank in enumerate(ranks):

                @pl.when(rank == 1)
                def _():
                    gather_further(t, s, way, h).wait_send()

                @pl.when(rank == 0)
                def _():
                    gather_other(t, s, way, h).wait_send()

                @pl.when(rank >= 1)
                def _():
                    gather_own(t, s, way, h).wait_send()

                for d in range(1, REACH):

                    @pl.when((rank <= REACH - d) & (rank >= 1))
                    def _():
                        gather_forward(t, s, way, d, h).wait_send()

    def share_copies():
        own, theirs = pl.ds(0, units), pl.ds(units, units)
        targets = (
            (gate_hbm, both.at[:, theirs]),
            (up_hbm, both.at[:, pl.ds(3 * units, units)]),
            (down_hbm, down.at[theirs]),
        )
        return [
            remote(src, dst, share_s.at[i], share_r.at[i], sibling)
            for i, (src, dst) in enumerate(targets)
        ]

    def place(k):
        return (k % half_rows), pl.ds((k // half_rows) * LANES, LANES)

    def compute(t, s, batch):
        owners = [(z + chips + k) % chips for k in BATCHES[batch]]
        count = len(owners) * half_rows

        def turning(shape, inner, outer):
            along = lax.broadcasted_iota(jnp.int32, shape, 0)
            across = lax.broadcasted_iota(jnp.int32, shape, 1)
            onehot = across == (along % outer) * inner + along // outer
            return onehot.astype(jnp.float32).astype(jnp.bfloat16)

        folded = [held[t, s, chip, :, 0:FOLD] for chip in owners]
        turned = jnp.dot(
            turning((chips * half_rows, count), half_rows, chips),
            jnp.concatenate(folded, axis=0),
            preferred_element_type=jnp.float32,
        )
        for k in range(folds):
            row, lanes = place(k)
            start = (k // half_rows) * LANES
            extra_in[0:chips, k * LANES : (k + 1) * LANES] = turned[
                row * chips : (row + 1) * chips, start : start + LANES
            ]
        tokens = [held[t, s, chip, :, FOLD : FOLD + width] for chip in owners]
        tokens = jnp.concatenate(tokens + [extra_in[...].astype(jnp.bfloat16)], axis=0)
        acts = jnp.dot(tokens, both[...], preferred_element_type=jnp.float32)
        gate_act, up_act = acts[:, : 2 * units], acts[:, 2 * units :]
        hidden = (gate_act * jax.nn.sigmoid(gate_act) * up_act).astype(jnp.bfloat16)

        def put_out(values, cols):
            values = values.astype(jnp.bfloat16)
            for i, chip in enumerate(owners):
                part[t, s, chip, :, cols] = values[i * half_rows : (i + 1) * half_rows]

        step = 2 * LANES
        for start in range(0, width, step):
            product = jnp.dot(
                hidden, down[:, pl.ds(start, step)], preferred_element_type=jnp.float32
            )
            for k in range(start // LANES, (start + step) // LANES):
                row, lanes = place(k)
                at = k * LANES - start
                extra_out[row * chips : (row + 1) * chips, lanes] = product[
                    count : count + chips, at : at + LANES
                ]
            put_out(product, pl.ds(FOLD + start, step))
        folded = jnp.dot(
            turning((count, chips * half_rows), chips, half_rows),
            extra_out[...].astype(jnp.bfloat16),
            preferred_element_type=jnp.float32,
        )
        put_out(folded, pl.ds(0, FOLD))

    def reduce_copy(t, s, way, d, h, dst, index, device):
        return remote(
            part.at[t, s, ahead(way, d), :, columns(h)],
            dst.at[:, columns(h)],
            r_s.at[way, t, s, index, h],
            r_r.at[way, t, s, index, h],
            device,
        )

    def reduce_on(t, s, way, d, h):
        return reduce_copy(t, s, way, d, h, sums.at[way, t, s, d - 1], d - 1, nexts[way])

    def reduce_out(t, s, way, d, h):
        device = nexts[way] if d == 1 else further[way]
        return reduce_copy(t, s, way, d, h, other_sum.at[t, s], REACH, device)

    def add_up(t, s, way, d, h):
        home, cols = ahead(way, d), columns(h)
        total = part[t, s, home, :, cols].astype(jnp.float32)
        total = total + sums[way, t, s, d, :, cols].astype(jnp.float32)
        part[t, s, home, :, cols] = total.astype(jnp.bfloat16)

    def start_reduce(t, s, d):
        for way, rank in enumerate(ranks):

            @pl.when(rank == group - 1)
            def _():
                for h in range(PIECES):
                    reduce_on(t, s, way, d, h).start()

    def reduce_step(t, s, start, hop, h):
        d = start - hop
        for way, rank in enumerate(ranks):

            @pl.when(rank == group - 1 - hop)
            def _():
                reduce_on(t, s, way, d + 1, h).wait_recv()
                if d >= 1:
                    add_up(t, s, way, d, h)
                    (reduce_on if hop < group - 1 else reduce_out)(t, s, way, d, h).start()

    def reduce_outside(t, s, h):
        for way, rank in enumerate(ranks):

            @pl.when(rank >= group - 2)
            def _():
                reduce_out(t, s, way, 1, h).wait_recv()

    def finish_reduce(t, s):
        for h in range(PIECES):
            for way, rank in enumerate(ranks):

                @pl.when(rank == group - 1)
                def _():
                    for d in range(REACH, 0, -1):
                        reduce_on(t, s, way, d, h).wait_send()

                for d in range(1, REACH):

                    @pl.when((rank >= d - 2) & (rank < group - 1) & (rank >= 1))
                    def _():
                        reduce_on(t, s, way, d, h).wait_send()

                @pl.when(rank == 0)
                def _():
                    reduce_out(t, s, way, 2, h).wait_send()
                    reduce_out(t, s, way, 1, h).wait_send()

    def packing(t, s):
        along = lax.broadcasted_iota(jnp.int32, (rows, rows), 0)
        across = lax.broadcasted_iota(jnp.int32, (rows, rows), 1)

        def column(row):
            spread = jnp.broadcast_to(row, (rows, rows))
            return jnp.sum(jnp.where(across == along, spread, 0.0), axis=1, keepdims=True)

        named = routes[s][t].astype(jnp.float32)
        away = jnp.abs(named - own_expert)
        before = jnp.where(along < across, jnp.broadcast_to(column(away), (rows, rows)), 0.0)
        before = jnp.sum(before, axis=0, keepdims=True)
        index = lax.broadcasted_iota(jnp.int32, (1, rows), 1).astype(jnp.float32)
        order = jnp.where(away > 0.5, before, index - before)
        spare = jnp.where(away > 0.5, half_rows - 1.0, rows - 1.0)
        put = jnp.where(order < half_rows, order + half_rows * away, spare)
        return along, across, named, put, column(put), jnp.sum(away, axis=1, keepdims=True)

    def prepare(t, s):
        along, across, named, put, _, _ = packing(t, s)
        onehot = (along.astype(jnp.float32) == put).astype(jnp.float32)
        chosen = jnp.sum(onehot * named, axis=1, keepdims=True)
        packed = jnp.dot(
            onehot.astype(jnp.bfloat16), current[s], preferred_element_type=jnp.float32
        )
        current[s] = packed.astype(jnp.bfloat16)
        for h in range(2):
            widened = packed[h * half_rows : (h + 1) * half_rows]
            mean = jnp.mean(widened * widened, axis=-1, keepdims=True)
            normed = widened * lax.rsqrt(mean + epsilon) * gains[...]
            normed = normed.astype(jnp.bfloat16)
            if h == 0:
                held[t, s, z, :, FOLD : FOLD + width] = normed
            else:
                other[t, s, :, FOLD : FOLD + width] = normed
            normed = normed.astype(jnp.float32)
            for k in range(folds):
                row, lanes = place(k)
                fold[1 - h, row : row + 1, lanes] = normed[
                    half_rows - 1 : half_rows, k * LANES : (k + 1) * LANES
                ]
            part_of = chosen[h * half_rows : (h + 1) * half_rows]
            column = jnp.where(part_of < 0.5, router[0:1], router[1:2])
            score = jnp.sum(normed * column, axis=1, keepdims=True)
            weight[s, h * half_rows : (h + 1) * half_rows] = jnp.broadcast_to(
                route_scale * jax.nn.sigmoid(score), (half_rows, LANES)
            )
        held[t, s, z, :, 0:FOLD] = fold[0].astype(jnp.bfloat16)
        other[t, s, :, 0:FOLD] = fold[1].astype(jnp.bfloat16)

    def main_columns(h):
        first = max(h * piece, FOLD) - FOLD
        return first, (h + 1) * piece - FOLD

    def pipe_copy(s, h):
        first, last = main_columns(h)
        cols = pl.ds(first, last - first)
        return remote(
            outs[s].at[0, :, cols],
            arrived.at[s, :, cols],
            pipe_s.at[s, h],
            pipe_r.at[s, h],
            onward if s == 0 else backward,
        )

    def receive(s):
        for h in range(PIECES):
            pipe_copy(s, h).wait_recv()
        current[s] = arrived[s]

        @pl.when(p == (0 if s == 0 else sections - 1))
        def _():
            current[s] = enters[s][0]

    def finalize(t, s, h):
        _, across, _, _, put, load = packing(t, s)
        first, last = main_columns(h)

        def sums_of(cols):
            total = part[t, s, z, :, cols].astype(jnp.float32)
            total = total + sums[0, t, s, 0, :, cols].astype(jnp.float32)
            total = total + sums[1, t, s, 0, :, cols].astype(jnp.float32)
            return total, other_sum[t, s, :, cols].astype(jnp.float32)

        if h == 0:
            fold_sum[0], fold_sum[1] = sums_of(pl.ds(0, FOLD))
        crowded = (load > half_rows + 0.5, load < half_rows - 0.5)
        both_sums = sums_of(pl.ds(FOLD + first, last - first))
        for b in range(2):
            outcome[b * half_rows : (b + 1) * half_rows, first:last] = both_sums[b]
            end = (b + 1) * half_rows - 1
            for k in range(first // LANES, last // LANES):
                row, lanes = place(k)
                here = pl.ds(k * LANES, LANES)
                outcome[end : end + 1, here] = jnp.where(
                    crowded[b], fold_sum[1 - b, row : row + 1, lanes], outcome[end : end + 1, here]
                )
        widened = current[s, :, first:last].astype(jnp.float32)
        result = widened + weight[s, :, 0:1] * outcome[:, first:last]
        back = (across.astype(jnp.float32) == put).astype(jnp.float32).astype(jnp.bfloat16)
        result = jnp.dot(back, result.astype(jnp.bfloat16), preferred_element_type=jnp.float32)
        outs[s][t, :, first:last] = result.astype(jnp.bfloat16)
        if t == 0:
            pipe_copy(s, h).start()

    barrier = pltpu.get_barrier_semaphore()
    partners = (above, below, sibling, onward, backward) + further
    for partner in partners:
        pl.semaphore_signal(barrier, inc=1, device_id=partner, device_id_type=MESH)
    loads = (
        pltpu.make_async_copy(gate_hbm, both.at[:, pl.ds(0, units)], load_sem.at[0]),
        pltpu.make_async_copy(up_hbm, both.at[:, pl.ds(2 * units, units)], load_sem.at[1]),
        pltpu.make_async_copy(down_hbm, down.at[pl.ds(0, units)], load_sem.at[2]),
    )
    for load in loads:
        load.start()
    fold[...] = jnp.zeros_like(fold)
    def clear():
        extra_in[...] = jnp.zeros_like(extra_in)
        extra_out[...] = jnp.zeros_like(extra_out)
        for way, rank in enumerate(ranks):

            @pl.when(rank == group - 1)
            def _():
                for t0 in range(2):
                    for s0 in range(2):
                        sums[way, t0, s0, 0] = jnp.zeros_like(sums[way, t0, s0, 0])

    entered = []
    for step, t, s, *at in ORDER:
        if step == PREPARE:
            if t == 0:
                current[s] = states[s][0]
            else:
                receive(s)
            prepare(t, s)
        elif step == START:
            if not entered:
                pl.semaphore_wait(barrier, len(partners))
            start_gather(t, s)
            if not entered:
                for copy in share_copies():
                    copy.start()
                clear()
            entered.append(step)
        elif step == GATHER:
            gather_step(t, s, *at)
        elif step == COMPUTE:
            if (t, s, *at) == (0, 0, 0):
                for load in loads:
                    load.wait()
                for copy in share_copies():
                    copy.wait()
            compute(t, s, *at)
        elif step == SENT:
            (finish_gather if at[0] == GATHER else finish_reduce)(t, s)
        elif step == TOTAL:
            start_reduce(t, s, *at)
        elif step == REDUCE:
            reduce_step(t, s, *at)
        elif step == OUTSIDE:
            reduce_outside(t, s, *at)
        else:
            finalize(t, s, *at)
    finish_reduce(1, 1)
    for s in range(2):
        for h in range(PIECES):
            pipe_copy(s, h).wait_send()


def hand_over(first, second, first_out, second_out):
    first_out[:, 0] = first[...]
    second_out[:, 0] = second[...]


def shards(
    first_state,
    second_state,
    first_enter,
    second_enter,
    norm_gain,
    router,
    gate_proj,
    up_proj,
    down_proj,
    first_routes,
    second_routes,
):
    chips = lax.axis_size("expert") // 2
    sections = lax.axis_size("pipe")
    rows, width = first_state.shape[1:]
    half_rows, across = rows // 2, width + FOLD
    units = gate_proj.shape[2]
    steps = first_routes.shape[0]
    vmem = pl.BlockSpec(memory_space=pltpu.VMEM)
    hbm = pl.BlockSpec(memory_space=pl.ANY)
    bf16 = jnp.bfloat16
    dma = pltpu.SemaphoreType.DMA
    out = jax.ShapeDtypeStruct((steps, rows, width), bf16)
    outs = pl.pallas_call(
        functools.partial(relay_kernel, chips, sections),
        out_shape=(out, out),
        in_specs=[vmem] * 6 + [hbm] * 3 + [vmem] * 2,
        out_specs=(vmem, vmem),
        scratch_shapes=[
            pltpu.VMEM((steps, 2, chips, half_rows, across), bf16),
            pltpu.VMEM((steps, 2, half_rows, across), bf16),
            pltpu.VMEM((steps, 2, chips, half_rows, across), bf16),
            pltpu.VMEM((2, steps, 2, REACH, half_rows, across), bf16),
            pltpu.VMEM((steps, 2, half_rows, across), bf16),
            pltpu.VMEM((2, rows, width), bf16),
            pltpu.VMEM((2, rows, width), bf16),
            pltpu.VMEM((2, rows, LANES), jnp.float32),
            pltpu.VMEM((width, 4 * units), bf16),
            pltpu.VMEM((2 * units, width), bf16),
            pltpu.VMEM((2, half_rows, FOLD), jnp.float32),
            pltpu.VMEM((rows, width), jnp.float32),
            pltpu.VMEM((2 * chips, width), jnp.float32),
            pltpu.VMEM((chips * half_rows, FOLD), jnp.float32),
            pltpu.VMEM((2, half_rows, FOLD), jnp.float32),
        ]
        + [dma((2, steps, 2, REACH + 1, PIECES))] * 4
        + [dma((3,))] * 2
        + [dma((2, PIECES))] * 2
        + [dma((3,))],
        compiler_params=pltpu.CompilerParams(
            collective_id=0, has_side_effects=True, vmem_limit_bytes=60 << 20
        ),
        name="relay_window",
    )(
        first_state,
        second_state,
        first_enter,
        second_enter,
        norm_gain,
        router[0].T,
        gate_proj[0],
        up_proj[0],
        down_proj[0],
        first_routes.reshape(steps, 1, rows),
        second_routes.reshape(steps, 1, rows),
    )
    whole = jax.ShapeDtypeStruct((steps, 1, rows, width), bf16)
    return pl.pallas_call(
        hand_over,
        out_shape=(whole, whole),
        in_specs=[vmem] * 2,
        out_specs=(vmem, vmem),
        name="hand_over",
    )(*outs)


def solution(mesh):
    return jax.shard_map(
        shards,
        mesh=mesh,
        in_specs=(
            P("pipe", "expert", None),
            P("pipe", "expert", None),
            P(None, "expert", None),
            P(None, "expert", None),
            P("pipe", None),
            P("pipe", None, None),
            P("pipe", None, "expert"),
            P("pipe", None, "expert"),
            P("pipe", "expert", None),
            P(None, "pipe", "expert", None),
            P(None, "pipe", "expert", None),
        ),
        out_specs=(P(None, "pipe", "expert", None), P(None, "pipe", "expert", None)),
        check_vma=False,
    )
```

```python
import functools

import jax
import jax.numpy as jnp
from jax import lax
from jax.experimental import pallas as pl
from jax.experimental.pallas import tpu as pltpu
from jax.sharding import PartitionSpec as P

EXP_WIN = 2
MESH = pl.DeviceIdType.MESH

epsilon = 1e-06
route_scale = 2.5

LANES = 128
FOLD = 256
REACH = 5
PIECES = 2
BATCHES = ((-2, -1, 0, 1, 2), (3, 4, 5))


PREPARE, START, GATHER, COMPUTE, TOTAL, REDUCE, OUTSIDE, SENT, FINISH = range(9)

ORDER = (
    (PREPARE, 0, 0),
    (START, 0, 0),
    (PREPARE, 0, 1),
    (GATHER, 0, 0, 1, 0),
    (GATHER, 0, 0, 1, 1),
    (START, 0, 1),
    (GATHER, 0, 0, 2, 0),
    (GATHER, 0, 0, 2, 1),
    (GATHER, 0, 1, 1, 0),
    (COMPUTE, 0, 0, 0),
    (GATHER, 0, 1, 1, 1),
    (TOTAL, 0, 0, 1),
    (TOTAL, 0, 0, 2),
    (GATHER, 0, 0, 3, 0),
    (GATHER, 0, 0, 3, 1),
    (GATHER, 0, 1, 2, 0),
    (GATHER, 0, 1, 2, 1),
    (REDUCE, 0, 0, 1, 1, 0),
    (COMPUTE, 0, 1, 0),
    (REDUCE, 0, 0, 1, 1, 1),
    (REDUCE, 0, 0, 2, 1, 0),
    (TOTAL, 0, 1, 1),
    (REDUCE, 0, 0, 2, 1, 1),
    (TOTAL, 0, 1, 2),
    (GATHER, 0, 0, 4, 0),
    (GATHER, 0, 0, 4, 1),
    (GATHER, 0, 1, 3, 0),
    (GATHER, 0, 1, 3, 1),
    (REDUCE, 0, 0, 2, 2, 0),
    (REDUCE, 0, 1, 1, 1, 0),
    (REDUCE, 0, 1, 1, 1, 1),
    (REDUCE, 0, 1, 2, 1, 0),
    (REDUCE, 0, 0, 2, 2, 1),
    (GATHER, 0, 0, 5, 0),
    (GATHER, 0, 0, 5, 1),
    (REDUCE, 0, 1, 2, 1, 1),
    (COMPUTE, 0, 0, 1),
    (TOTAL, 0, 0, 5),
    (TOTAL, 0, 0, 4),
    (GATHER, 0, 1, 4, 0),
    (GATHER, 0, 1, 4, 1),
    (REDUCE, 0, 1, 2, 2, 0),
    (SENT, 0, 0, GATHER),
    (REDUCE, 0, 0, 5, 1, 0),
    (REDUCE, 0, 0, 5, 1, 1),
    (TOTAL, 0, 0, 3),
    (REDUCE, 0, 1, 2, 2, 1),
    (GATHER, 0, 1, 5, 0),
    (GATHER, 0, 1, 5, 1),
    (COMPUTE, 0, 1, 1),
    (REDUCE, 0, 0, 4, 1, 0),
    (REDUCE, 0, 0, 4, 1, 1),
    (TOTAL, 0, 1, 5),
    (REDUCE, 0, 0, 5, 2, 0),
    (REDUCE, 0, 0, 5, 2, 1),
    (REDUCE, 0, 0, 3, 1, 0),
    (TOTAL, 0, 1, 4),
    (REDUCE, 0, 0, 3, 1, 1),
    (REDUCE, 0, 0, 4, 2, 0),
    (REDUCE, 0, 0, 4, 2, 1),
    (SENT, 0, 1, GATHER),
    (REDUCE, 0, 1, 5, 1, 0),
    (REDUCE, 0, 0, 5, 3, 0),
    (REDUCE, 0, 1, 5, 1, 1),
    (REDUCE, 0, 0, 5, 3, 1),
    (TOTAL, 0, 1, 3),
    (REDUCE, 0, 0, 3, 2, 0),
    (REDUCE, 0, 0, 3, 2, 1),
    (REDUCE, 0, 1, 4, 1, 0),
    (REDUCE, 0, 0, 4, 3, 0),
    (REDUCE, 0, 0, 4, 3, 1),
    (REDUCE, 0, 0, 3, 3, 0),
    (REDUCE, 0, 1, 4, 1, 1),
    (REDUCE, 0, 1, 5, 2, 0),
    (REDUCE, 0, 1, 5, 2, 1),
    (REDUCE, 0, 0, 3, 3, 1),
    (OUTSIDE, 0, 0, 0),
    (FINISH, 0, 0, 0),
    (OUTSIDE, 0, 0, 1),
    (REDUCE, 0, 1, 3, 1, 0),
    (REDUCE, 0, 1, 3, 1, 1),
    (REDUCE, 0, 1, 4, 2, 0),
    (REDUCE, 0, 1, 4, 2, 1),
    (FINISH, 0, 0, 1),
    (REDUCE, 0, 1, 5, 3, 0),
    (REDUCE, 0, 1, 5, 3, 1),
    (REDUCE, 0, 1, 3, 2, 0),
    (REDUCE, 0, 1, 3, 2, 1),
    (REDUCE, 0, 1, 4, 3, 0),
    (REDUCE, 0, 1, 4, 3, 1),
    (PREPARE, 1, 0),
    (REDUCE, 0, 1, 3, 3, 0),
    (REDUCE, 0, 1, 3, 3, 1),
    (OUTSIDE, 0, 1, 0),
    (OUTSIDE, 0, 1, 1),
    (FINISH, 0, 1, 0),
    (START, 1, 0),
    (FINISH, 0, 1, 1),
    (GATHER, 1, 0, 1, 0),
    (GATHER, 1, 0, 1, 1),
    (PREPARE, 1, 1),
    (START, 1, 1),
    (GATHER, 1, 0, 2, 0),
    (GATHER, 1, 0, 2, 1),
    (COMPUTE, 1, 0, 0),
    (GATHER, 1, 1, 1, 0),
    (GATHER, 1, 1, 1, 1),
    (TOTAL, 1, 0, 1),
    (TOTAL, 1, 0, 2),
    (GATHER, 1, 1, 2, 0),
    (GATHER, 1, 1, 2, 1),
    (SENT, 0, 0, REDUCE),
    (GATHER, 1, 0, 3, 0),
    (GATHER, 1, 0, 3, 1),
    (REDUCE, 1, 0, 1, 1, 0),
    (REDUCE, 1, 0, 1, 1, 1),
    (REDUCE, 1, 0, 2, 1, 0),
    (COMPUTE, 1, 1, 0),
    (TOTAL, 1, 1, 1),
    (TOTAL, 1, 1, 2),
    (SENT, 0, 1, REDUCE),
    (GATHER, 1, 1, 3, 0),
    (GATHER, 1, 1, 3, 1),
    (REDUCE, 1, 0, 2, 1, 1),
    (REDUCE, 1, 1, 1, 1, 0),
    (GATHER, 1, 0, 4, 0),
    (REDUCE, 1, 1, 1, 1, 1),
    (GATHER, 1, 0, 4, 1),
    (REDUCE, 1, 0, 2, 2, 0),
    (REDUCE, 1, 1, 2, 1, 0),
    (REDUCE, 1, 1, 2, 1, 1),
    (GATHER, 1, 1, 4, 0),
    (GATHER, 1, 1, 4, 1),
    (REDUCE, 1, 0, 2, 2, 1),
    (GATHER, 1, 0, 5, 0),
    (GATHER, 1, 0, 5, 1),
    (COMPUTE, 1, 0, 1),
    (TOTAL, 1, 0, 5),
    (TOTAL, 1, 0, 4),
    (REDUCE, 1, 1, 2, 2, 0),
    (REDUCE, 1, 1, 2, 2, 1),
    (GATHER, 1, 1, 5, 0),
    (SENT, 1, 0, GATHER),
    (REDUCE, 1, 0, 5, 1, 0),
    (GATHER, 1, 1, 5, 1),
    (REDUCE, 1, 0, 5, 1, 1),
    (COMPUTE, 1, 1, 1),
    (TOTAL, 1, 1, 5),
    (TOTAL, 1, 1, 4),
    (TOTAL, 1, 0, 3),
    (SENT, 1, 1, GATHER),
    (REDUCE, 1, 1, 5, 1, 0),
    (REDUCE, 1, 1, 5, 1, 1),
    (TOTAL, 1, 1, 3),
    (REDUCE, 1, 0, 4, 1, 0),
    (REDUCE, 1, 0, 4, 1, 1),
    (REDUCE, 1, 1, 4, 1, 0),
    (REDUCE, 1, 1, 4, 1, 1),
    (REDUCE, 1, 0, 5, 2, 0),
    (REDUCE, 1, 0, 5, 2, 1),
    (REDUCE, 1, 0, 3, 1, 0),
    (REDUCE, 1, 1, 5, 2, 0),
    (REDUCE, 1, 1, 5, 2, 1),
    (REDUCE, 1, 0, 3, 1, 1),
    (REDUCE, 1, 0, 4, 2, 0),
    (REDUCE, 1, 0, 4, 2, 1),
    (REDUCE, 1, 1, 3, 1, 0),
    (REDUCE, 1, 1, 3, 1, 1),
    (REDUCE, 1, 1, 4, 2, 0),
    (REDUCE, 1, 0, 5, 3, 0),
    (REDUCE, 1, 1, 4, 2, 1),
    (REDUCE, 1, 0, 5, 3, 1),
    (REDUCE, 1, 0, 3, 2, 0),
    (REDUCE, 1, 1, 5, 3, 0),
    (REDUCE, 1, 0, 3, 2, 1),
    (REDUCE, 1, 1, 5, 3, 1),
    (REDUCE, 1, 1, 3, 2, 0),
    (REDUCE, 1, 1, 3, 2, 1),
    (REDUCE, 1, 0, 4, 3, 0),
    (REDUCE, 1, 0, 4, 3, 1),
    (REDUCE, 1, 1, 4, 3, 0),
    (REDUCE, 1, 1, 4, 3, 1),
    (REDUCE, 1, 0, 3, 3, 0),
    (REDUCE, 1, 0, 3, 3, 1),
    (OUTSIDE, 1, 0, 0),
    (OUTSIDE, 1, 0, 1),
    (REDUCE, 1, 1, 3, 3, 0),
    (FINISH, 1, 0, 0),
    (FINISH, 1, 0, 1),
    (OUTSIDE, 1, 1, 0),
    (FINISH, 1, 1, 0),
    (SENT, 1, 0, REDUCE),
    (REDUCE, 1, 1, 3, 3, 1),
    (OUTSIDE, 1, 1, 1),
    (FINISH, 1, 1, 1),
)


def relay_kernel(
    chips,
    sections,
    first_state,
    second_state,
    first_enter,
    second_enter,
    gains,
    router,
    gate_hbm,
    up_hbm,
    down_hbm,
    first_routes,
    second_routes,
    first_out,
    second_out,
    held,
    other,
    part,
    sums,
    other_sum,
    arrived,
    current,
    weight,
    both,
    down,
    fold,
    outcome,
    extra_in,
    extra_out,
    fold_sum,
    g_s,
    g_r,
    r_s,
    r_r,
    share_s,
    share_r,
    pipe_s,
    pipe_r,
    load_sem,
):
    rows, width = current.shape[1:]
    half_rows = rows // 2
    units = gate_hbm.shape[1]
    folds = width // LANES
    piece = (width + FOLD) // PIECES
    group = chips // EXP_WIN
    e = lax.axis_index("expert")
    p = lax.axis_index("pipe")
    z, c = e // 2, e % 2
    own_expert = (z // group).astype(jnp.float32)
    above = {"expert": ((z + 1) % chips) * 2 + c}
    below = {"expert": ((z + chips - 1) % chips) * 2 + c}
    sibling = {"expert": z * 2 + (1 - c)}
    further = (
        {"expert": ((z + chips - 2) % chips) * 2 + c},
        {"expert": ((z + 2) % chips) * 2 + c},
    )
    onward = {"pipe": (p + 1) % sections}
    backward = {"pipe": (p + sections - 1) % sections}
    nexts = (below, above)
    ranks = (z % group, group - 1 - z % group)
    routes = (first_routes, second_routes)
    states = (first_state, second_state)
    enters = (first_enter, second_enter)
    outs = (first_out, second_out)

    def ahead(way, distance):
        return (z + (chips - distance if way == 0 else distance)) % chips

    def behind(way, distance):
        return ahead(1 - way, distance)

    def remote(src, dst, send, recv, device):
        return pltpu.make_async_remote_copy(
            src_ref=src,
            dst_ref=dst,
            send_sem=send,
            recv_sem=recv,
            device_id=device,
            device_id_type=MESH,
        )

    def columns(h):
        return pl.ds(h * piece, piece)

    def gather_copy(t, s, way, src, chip, index, h, device):
        return remote(
            src.at[:, columns(h)],
            held.at[t, s, chip, :, columns(h)],
            g_s.at[way, t, s, index, h],
            g_r.at[way, t, s, index, h],
            device,
        )

    def gather_own(t, s, way, h):
        return gather_copy(t, s, way, held.at[t, s, z], z, 1, h, nexts[way])

    def gather_other(t, s, way, h):
        return gather_copy(t, s, way, other.at[t, s], z, 1, h, nexts[way])

    def gather_further(t, s, way, h):
        return gather_copy(t, s, way, other.at[t, s], z, 2, h, further[way])

    def gather_forward(t, s, way, d, h):
        chip = behind(way, d)
        return gather_copy(t, s, way, held.at[t, s, chip], chip, d + 1, h, nexts[way])

    def gather_arrival(t, s, way, d, h):
        chip = behind(way, d)
        return gather_copy(t, s, way, held.at[t, s, chip], chip, d, h, nexts[way])

    def start_gather(t, s):
        for h in range(PIECES):
            for way, rank in enumerate(ranks):

                @pl.when(rank == 1)
                def _():
                    gather_further(t, s, way, h).start()

                @pl.when(rank == 0)
                def _():
                    gather_other(t, s, way, h).start()

                @pl.when(rank >= 1)
                def _():
                    gather_own(t, s, way, h).start()

    def gather_step(t, s, d, h):
        for way, rank in enumerate(ranks):

            @pl.when(rank <= REACH - d)
            def _():
                gather_arrival(t, s, way, d, h).wait_recv()
                if d < REACH:

                    @pl.when(rank >= 1)
                    def _():
                        gather_forward(t, s, way, d, h).start()

    def finish_gather(t, s):
        for h in range(PIECES):
            for way, rank in enumerate(ranks):

                @pl.when(rank == 1)
                def _():
                    gather_further(t, s, way, h).wait_send()

                @pl.when(rank == 0)
                def _():
                    gather_other(t, s, way, h).wait_send()

                @pl.when(rank >= 1)
                def _():
                    gather_own(t, s, way, h).wait_send()

                for d in range(1, REACH):

                    @pl.when((rank <= REACH - d) & (rank >= 1))
                    def _():
                        gather_forward(t, s, way, d, h).wait_send()

    def share_copies():
        own, theirs = pl.ds(0, units), pl.ds(units, units)
        targets = (
            (gate_hbm, both.at[:, theirs]),
            (up_hbm, both.at[:, pl.ds(3 * units, units)]),
            (down_hbm, down.at[theirs]),
        )
        return [
            remote(src, dst, share_s.at[i], share_r.at[i], sibling)
            for i, (src, dst) in enumerate(targets)
        ]

    def place(k):
        return (k % half_rows), pl.ds((k // half_rows) * LANES, LANES)

    def compute(t, s, batch):
        owners = [(z + chips + k) % chips for k in BATCHES[batch]]
        count = len(owners) * half_rows

        def turning(shape, inner, outer):
            along = lax.broadcasted_iota(jnp.int32, shape, 0)
            across = lax.broadcasted_iota(jnp.int32, shape, 1)
            onehot = across == (along % outer) * inner + along // outer
            return onehot.astype(jnp.float32).astype(jnp.bfloat16)

        folded = [held[t, s, chip, :, 0:FOLD] for chip in owners]
        turned = jnp.dot(
            turning((chips * half_rows, count), half_rows, chips),
            jnp.concatenate(folded, axis=0),
            preferred_element_type=jnp.float32,
        )
        for k in range(folds):
            row, lanes = place(k)
            start = (k // half_rows) * LANES
            extra_in[0:chips, k * LANES : (k + 1) * LANES] = turned[
                row * chips : (row + 1) * chips, start : start + LANES
            ]
        tokens = [held[t, s, chip, :, FOLD : FOLD + width] for chip in owners]
        tokens = jnp.concatenate(tokens + [extra_in[...].astype(jnp.bfloat16)], axis=0)
        acts = jnp.dot(tokens, both[...], preferred_element_type=jnp.float32)
        gate_act, up_act = acts[:, : 2 * units], acts[:, 2 * units :]
        hidden = (gate_act * jax.nn.sigmoid(gate_act) * up_act).astype(jnp.bfloat16)

        def put_out(values, cols):
            values = values.astype(jnp.bfloat16)
            for i, chip in enumerate(owners):
                part[t, s, chip, :, cols] = values[i * half_rows : (i + 1) * half_rows]

        step = 2 * LANES
        for start in range(0, width, step):
            product = jnp.dot(
                hidden, down[:, pl.ds(start, step)], preferred_element_type=jnp.float32
            )
            for k in range(start // LANES, (start + step) // LANES):
                row, lanes = place(k)
                at = k * LANES - start
                extra_out[row * chips : (row + 1) * chips, lanes] = product[
                    count : count + chips, at : at + LANES
                ]
            put_out(product, pl.ds(FOLD + start, step))
        folded = jnp.dot(
            turning((count, chips * half_rows), chips, half_rows),
            extra_out[...].astype(jnp.bfloat16),
            preferred_element_type=jnp.float32,
        )
        put_out(folded, pl.ds(0, FOLD))

    def reduce_copy(t, s, way, d, h, dst, index, device):
        return remote(
            part.at[t, s, ahead(way, d), :, columns(h)],
            dst.at[:, columns(h)],
            r_s.at[way, t, s, index, h],
            r_r.at[way, t, s, index, h],
            device,
        )

    def reduce_on(t, s, way, d, h):
        return reduce_copy(t, s, way, d, h, sums.at[way, t, s, d - 1], d - 1, nexts[way])

    def reduce_out(t, s, way, d, h):
        device = nexts[way] if d == 1 else further[way]
        return reduce_copy(t, s, way, d, h, other_sum.at[t, s], REACH, device)

    def add_up(t, s, way, d, h):
        home, cols = ahead(way, d), columns(h)
        total = part[t, s, home, :, cols].astype(jnp.float32)
        total = total + sums[way, t, s, d, :, cols].astype(jnp.float32)
        part[t, s, home, :, cols] = total.astype(jnp.bfloat16)

    def start_reduce(t, s, d):
        for way, rank in enumerate(ranks):

            @pl.when(rank == group - 1)
            def _():
                for h in range(PIECES):
                    reduce_on(t, s, way, d, h).start()

    def reduce_step(t, s, start, hop, h):
        d = start - hop
        for way, rank in enumerate(ranks):

            @pl.when(rank == group - 1 - hop)
            def _():
                reduce_on(t, s, way, d + 1, h).wait_recv()
                if d >= 1:
                    add_up(t, s, way, d, h)
                    (reduce_on if hop < group - 1 else reduce_out)(t, s, way, d, h).start()

    def reduce_outside(t, s, h):
        for way, rank in enumerate(ranks):

            @pl.when(rank >= group - 2)
            def _():
                reduce_out(t, s, way, 1, h).wait_recv()

    def finish_reduce(t, s):
        for h in range(PIECES):
            for way, rank in enumerate(ranks):

                @pl.when(rank == group - 1)
                def _():
                    for d in range(REACH, 0, -1):
                        reduce_on(t, s, way, d, h).wait_send()

                for d in range(1, REACH):

                    @pl.when((rank >= d - 2) & (rank < group - 1) & (rank >= 1))
                    def _():
                        reduce_on(t, s, way, d, h).wait_send()

                @pl.when(rank == 0)
                def _():
                    reduce_out(t, s, way, 2, h).wait_send()
                    reduce_out(t, s, way, 1, h).wait_send()

    def packing(t, s):
        along = lax.broadcasted_iota(jnp.int32, (rows, rows), 0)
        across = lax.broadcasted_iota(jnp.int32, (rows, rows), 1)

        def column(row):
            spread = jnp.broadcast_to(row, (rows, rows))
            return jnp.sum(jnp.where(across == along, spread, 0.0), axis=1, keepdims=True)

        named = routes[s][t].astype(jnp.float32)
        away = jnp.abs(named - own_expert)
        before = jnp.where(along < across, jnp.broadcast_to(column(away), (rows, rows)), 0.0)
        before = jnp.sum(before, axis=0, keepdims=True)
        index = lax.broadcasted_iota(jnp.int32, (1, rows), 1).astype(jnp.float32)
        order = jnp.where(away > 0.5, before, index - before)
        spare = jnp.where(away > 0.5, half_rows - 1.0, rows - 1.0)
        put = jnp.where(order < half_rows, order + half_rows * away, spare)
        return along, across, named, put, column(put), jnp.sum(away, axis=1, keepdims=True)

    def prepare(t, s):
        along, across, named, put, _, _ = packing(t, s)
        onehot = (along.astype(jnp.float32) == put).astype(jnp.float32)
        chosen = jnp.sum(onehot * named, axis=1, keepdims=True)
        packed = jnp.dot(
            onehot.astype(jnp.bfloat16), current[s], preferred_element_type=jnp.float32
        )
        current[s] = packed.astype(jnp.bfloat16)
        for h in range(2):
            widened = packed[h * half_rows : (h + 1) * half_rows]
            mean = jnp.mean(widened * widened, axis=-1, keepdims=True)
            normed = widened * lax.rsqrt(mean + epsilon) * gains[...]
            normed = normed.astype(jnp.bfloat16)
            if h == 0:
                held[t, s, z, :, FOLD : FOLD + width] = normed
            else:
                other[t, s, :, FOLD : FOLD + width] = normed
            normed = normed.astype(jnp.float32)
            for k in range(folds):
                row, lanes = place(k)
                fold[1 - h, row : row + 1, lanes] = normed[
                    half_rows - 1 : half_rows, k * LANES : (k + 1) * LANES
                ]
            part_of = chosen[h * half_rows : (h + 1) * half_rows]
            column = jnp.where(part_of < 0.5, router[0:1], router[1:2])
            score = jnp.sum(normed * column, axis=1, keepdims=True)
            weight[s, h * half_rows : (h + 1) * half_rows] = jnp.broadcast_to(
                route_scale * jax.nn.sigmoid(score), (half_rows, LANES)
            )
        held[t, s, z, :, 0:FOLD] = fold[0].astype(jnp.bfloat16)
        other[t, s, :, 0:FOLD] = fold[1].astype(jnp.bfloat16)

    def main_columns(h):
        first = max(h * piece, FOLD) - FOLD
        return first, (h + 1) * piece - FOLD

    def pipe_copy(s, h):
        first, last = main_columns(h)
        cols = pl.ds(first, last - first)
        return remote(
            outs[s].at[0, :, cols],
            arrived.at[s, :, cols],
            pipe_s.at[s, h],
            pipe_r.at[s, h],
            onward if s == 0 else backward,
        )

    def receive(s):
        for h in range(PIECES):
            pipe_copy(s, h).wait_recv()
        current[s] = arrived[s]

        @pl.when(p == (0 if s == 0 else sections - 1))
        def _():
            current[s] = enters[s][0]

    def finalize(t, s, h):
        _, across, _, _, put, load = packing(t, s)
        first, last = main_columns(h)

        def sums_of(cols):
            total = part[t, s, z, :, cols].astype(jnp.float32)
            total = total + sums[0, t, s, 0, :, cols].astype(jnp.float32)
            total = total + sums[1, t, s, 0, :, cols].astype(jnp.float32)
            return total, other_sum[t, s, :, cols].astype(jnp.float32)

        if h == 0:
            fold_sum[0], fold_sum[1] = sums_of(pl.ds(0, FOLD))
        crowded = (load > half_rows + 0.5, load < half_rows - 0.5)
        both_sums = sums_of(pl.ds(FOLD + first, last - first))
        for b in range(2):
            outcome[b * half_rows : (b + 1) * half_rows, first:last] = both_sums[b]
            end = (b + 1) * half_rows - 1
            for k in range(first // LANES, last // LANES):
                row, lanes = place(k)
                here = pl.ds(k * LANES, LANES)
                outcome[end : end + 1, here] = jnp.where(
                    crowded[b], fold_sum[1 - b, row : row + 1, lanes], outcome[end : end + 1, here]
                )
        widened = current[s, :, first:last].astype(jnp.float32)
        result = widened + weight[s, :, 0:1] * outcome[:, first:last]
        back = (across.astype(jnp.float32) == put).astype(jnp.float32).astype(jnp.bfloat16)
        result = jnp.dot(back, result.astype(jnp.bfloat16), preferred_element_type=jnp.float32)
        outs[s][t, :, first:last] = result.astype(jnp.bfloat16)
        if t == 0:
            pipe_copy(s, h).start()

    barrier = pltpu.get_barrier_semaphore()
    partners = (above, below, sibling, onward, backward) + further
    for partner in partners:
        pl.semaphore_signal(barrier, inc=1, device_id=partner, device_id_type=MESH)
    loads = (
        pltpu.make_async_copy(gate_hbm, both.at[:, pl.ds(0, units)], load_sem.at[0]),
        pltpu.make_async_copy(up_hbm, both.at[:, pl.ds(2 * units, units)], load_sem.at[1]),
        pltpu.make_async_copy(down_hbm, down.at[pl.ds(0, units)], load_sem.at[2]),
    )
    for load in loads:
        load.start()
    fold[...] = jnp.zeros_like(fold)
    def clear():
        extra_in[...] = jnp.zeros_like(extra_in)
        extra_out[...] = jnp.zeros_like(extra_out)
        for way, rank in enumerate(ranks):

            @pl.when(rank == group - 1)
            def _():
                for t0 in range(2):
                    for s0 in range(2):
                        sums[way, t0, s0, 0] = jnp.zeros_like(sums[way, t0, s0, 0])

    entered = []
    for step, t, s, *at in ORDER:
        if step == PREPARE:
            if t == 0:
                current[s] = states[s][0]
            else:
                receive(s)
            prepare(t, s)
        elif step == START:
            if not entered:
                pl.semaphore_wait(barrier, len(partners))
            start_gather(t, s)
            if not entered:
                for copy in share_copies():
                    copy.start()
                clear()
            entered.append(step)
        elif step == GATHER:
            gather_step(t, s, *at)
        elif step == COMPUTE:
            if (t, s, *at) == (0, 0, 0):
                for load in loads:
                    load.wait()
                for copy in share_copies():
                    copy.wait()
            compute(t, s, *at)
        elif step == SENT:
            (finish_gather if at[0] == GATHER else finish_reduce)(t, s)
        elif step == TOTAL:
            start_reduce(t, s, *at)
        elif step == REDUCE:
            reduce_step(t, s, *at)
        elif step == OUTSIDE:
            reduce_outside(t, s, *at)
        else:
            finalize(t, s, *at)
    finish_reduce(1, 1)
    for s in range(2):
        for h in range(PIECES):
            pipe_copy(s, h).wait_send()


def hand_over(first, second, first_out, second_out):
    first_out[0] = first[...]
    second_out[0] = second[...]


def shards(
    first_state,
    second_state,
    first_enter,
    second_enter,
    norm_gain,
    router,
    gate_proj,
    up_proj,
    down_proj,
    first_routes,
    second_routes,
):
    chips = lax.axis_size("expert") // 2
    sections = lax.axis_size("pipe")
    rows, width = first_state.shape[1:]
    half_rows, across = rows // 2, width + FOLD
    units = gate_proj.shape[2]
    steps = first_routes.shape[0]
    vmem = pl.BlockSpec(memory_space=pltpu.VMEM)
    hbm = pl.BlockSpec(memory_space=pl.ANY)
    bf16 = jnp.bfloat16
    dma = pltpu.SemaphoreType.DMA
    out = jax.ShapeDtypeStruct((steps, rows, width), bf16)
    outs = pl.pallas_call(
        functools.partial(relay_kernel, chips, sections),
        out_shape=(out, out),
        in_specs=[vmem] * 6 + [hbm] * 3 + [vmem] * 2,
        out_specs=(vmem, vmem),
        scratch_shapes=[
            pltpu.VMEM((steps, 2, chips, half_rows, across), bf16),
            pltpu.VMEM((steps, 2, half_rows, across), bf16),
            pltpu.VMEM((steps, 2, chips, half_rows, across), bf16),
            pltpu.VMEM((2, steps, 2, REACH, half_rows, across), bf16),
            pltpu.VMEM((steps, 2, half_rows, across), bf16),
            pltpu.VMEM((2, rows, width), bf16),
            pltpu.VMEM((2, rows, width), bf16),
            pltpu.VMEM((2, rows, LANES), jnp.float32),
            pltpu.VMEM((width, 4 * units), bf16),
            pltpu.VMEM((2 * units, width), bf16),
            pltpu.VMEM((2, half_rows, FOLD), jnp.float32),
            pltpu.VMEM((rows, width), jnp.float32),
            pltpu.VMEM((2 * chips, width), jnp.float32),
            pltpu.VMEM((chips * half_rows, FOLD), jnp.float32),
            pltpu.VMEM((2, half_rows, FOLD), jnp.float32),
        ]
        + [dma((2, steps, 2, REACH + 1, PIECES))] * 4
        + [dma((3,))] * 2
        + [dma((2, PIECES))] * 2
        + [dma((3,))],
        compiler_params=pltpu.CompilerParams(
            collective_id=0, has_side_effects=True, vmem_limit_bytes=60 << 20
        ),
        name="relay_window",
    )(
        first_state,
        second_state,
        first_enter,
        second_enter,
        norm_gain,
        router[0].T,
        gate_proj[0],
        up_proj[0],
        down_proj[0],
        first_routes.reshape(steps, 1, rows),
        second_routes.reshape(steps, 1, rows),
    )
    whole = jax.ShapeDtypeStruct((steps, 1, rows, width), bf16)
    given = pl.BlockSpec((1, rows, width), lambda step: (step, 0, 0))
    result = pl.BlockSpec((1, 1, rows, width), lambda step: (step, 0, 0, 0))
    return pl.pallas_call(
        hand_over,
        grid=(steps,),
        out_shape=(whole, whole),
        in_specs=[given] * 2,
        out_specs=(result, result),
        name="hand_over",
    )(*outs)


def solution(mesh):
    return jax.shard_map(
        shards,
        mesh=mesh,
        in_specs=(
            P("pipe", "expert", None),
            P("pipe", "expert", None),
            P(None, "expert", None),
            P(None, "expert", None),
            P("pipe", None),
            P("pipe", None, None),
            P("pipe", None, "expert"),
            P("pipe", None, "expert"),
            P("pipe", "expert", None),
            P(None, "pipe", "expert", None),
            P(None, "pipe", "expert", None),
        ),
        out_specs=(P(None, "pipe", "expert", None), P(None, "pipe", "expert", None)),
        check_vma=False,
    )
```
